512 devices in a mesh: tile: 128 (over y, z_hi, x, core), mp: 4 (over z_lo).
Axes of the slice: x: 4, y: 8, z: 8 (z_hi: 2, z_lo: 4; z = z_hi * 4 + z_lo), core: 2. Of those that a mesh axis runs over, the one named last changes fastest.
Arguments:
- query: bfloat16 [32768, 1536], P('tile', 'mp'), may hold values from -28 to 28
- key: bfloat16 [32768, 1536], P('tile', 'mp'), may hold values from -6 to 6
- value: bfloat16 [32768, 1536], P('tile', 'mp'), may hold values from -6 to 6
- grad_y: bfloat16 [32768, 3072], P('tile', 'mp'), may hold values from -12 to 12
- w_out: bfloat16 [3072, 1536], P('tile', 'mp'), may hold values from -0.109375 to 0.109375
Outputs:
- grad_query: bfloat16 [32768, 1536], P('tile', 'mp')
- grad_key: bfloat16 [32768, 1536], P('tile', 'mp')
- grad_value: bfloat16 [32768, 1536], P('tile', 'mp')
The draws below stay inside these ranges and needn't reach their ends.
All inputs are finite; a program needn't handle non-finite values.
Results may differ from the reference program's by a relative error of at most 0.0095.
Values may be sent and summed in bfloat16 or wider, within the bound.
A program may use at most 64 MiB of HBM per device.

```python
import jax
import jax.numpy as jnp
from jax import lax

D = 3072
HEADS = 12
HD = 128
BAND = 8
TILE_COLS = 8
TH = 16
TW = 16
TOK_DEV = 256
TOKENS = 32768
FEAT = 1536
N_TILE = 128


def draw_query(key, part):
    key = jax.random.fold_in(key, 3)
    second_key = jax.random.fold_in(key, 1)
    base = jnp.clip(jax.random.normal(second_key, (TOKENS, FEAT), jnp.float32), -4.0, 4.0) * 1.5
    return base.astype(jnp.bfloat16)


def draw_key(key, part):
    key = jax.random.fold_in(key, 5)
    second_key = jax.random.fold_in(key, 1)
    base = jnp.clip(jax.random.normal(second_key, (TOKENS, FEAT), jnp.float32), -6.0, 6.0)
    return base.astype(jnp.bfloat16)


def block_scale(own_key, extent, cuts, smallest, high):
    loudness, own = 1.0, jax.random.fold_in(own_key, 6)
    for dim, blocks in cuts:
        steps = jnp.exp(jax.random.uniform(jax.random.fold_in(own, dim), (blocks,), jnp.float32, smallest / len(cuts), high / len(cuts)))
        loudness = loudness * jnp.repeat(steps, extent[dim] // blocks).reshape([-1 if axis == dim else 1 for axis in range(len(extent))])
    return loudness


def normal_values(stream_key, dims, scale, reach, cuts=(), held_as=jnp.bfloat16):
    level = block_scale(stream_key, dims, cuts, -0.22, 0.18) if cuts else 1.0
    values = jax.random.normal(stream_key, dims, jnp.float32) * scale * level
    return jnp.minimum(jnp.maximum(values, -reach), reach).astype(held_as)


def setup_inputs(seed: int = 0) -> dict:
    key_list = jax.random.split(jax.random.key(seed), 6)
    query = draw_query(jax.random.fold_in(key_list[5], 71), 0)
    key = draw_key(jax.random.fold_in(key_list[5], 71), 0)
    value = normal_values(key_list[2], (TOKENS, FEAT), 1.0, 6.0, ((0, 128), (1, 4)))
    grad_y = normal_values(key_list[3], (TOKENS, D), 2.0, 12.0, ((0, 128), (1, 4)))
    w_out = normal_values(key_list[4], (D, FEAT), D ** -0.5, 0.109375, ((0, 128), (1, 4)))
    return dict(query=query, key=key, value=value, grad_y=grad_y, w_out=w_out)


def narrowed(values):
    return lax.optimization_barrier(values.astype(jnp.bfloat16)).astype(jnp.float32)


def reference(query, key, value, grad_y, w_out):
    grid_rows = N_TILE // TILE_COLS
    features = HEADS * HD
    cotangent = jnp.dot(grad_y, w_out, preferred_element_type=jnp.float32).astype(jnp.bfloat16)

    def to_image(tokens_in):
        shaped = tokens_in.reshape(grid_rows, TILE_COLS, TH, TW, features)
        return shaped.transpose(0, 2, 1, 3, 4).reshape(grid_rows * TH, TILE_COLS * TW, features)

    padding = ((BAND, BAND), (BAND, BAND), (0, 0))
    key_image = jnp.pad(to_image(key), padding)
    value_image = jnp.pad(to_image(value), padding)
    inside = jnp.pad(jnp.ones((grid_rows * TH, TILE_COLS * TW), jnp.float32), ((BAND, BAND), (BAND, BAND)))
    window_rows = TH + 2 * BAND
    window_cols = TW + 2 * BAND
    score_scale = HD ** -0.5
    tiles_query = query.reshape(N_TILE, TOK_DEV, HEADS, HD)
    tiles_cotan = cotangent.reshape(N_TILE, TOK_DEV, HEADS, HD)
    zeros_image = jnp.zeros(key_image.shape, jnp.float32)

    def tile_step(images, inputs):
        key_grad_image, value_grad_image = images
        tile_index, query_tile, cotan_tile = inputs
        row_start = (tile_index // TILE_COLS) * TH
        col_start = (tile_index % TILE_COLS) * TW
        zero_index = tile_index * 0
        starts = (row_start, col_start, zero_index)
        sizes = (window_rows, window_cols, features)
        keys_win = lax.dynamic_slice(key_image, starts, sizes).reshape(window_rows * window_cols, HEADS, HD)
        values_win = lax.dynamic_slice(value_image, starts, sizes).reshape(window_rows * window_cols, HEADS, HD)
        key_valid = lax.dynamic_slice(inside, (row_start, col_start), (window_rows, window_cols)).reshape(-1) > 0.5
        query_wide = query_tile.astype(jnp.float32)
        cotan_wide = cotan_tile.astype(jnp.float32)
        keys_wide = keys_win.astype(jnp.float32)
        values_wide = values_win.astype(jnp.float32)
        scores = jnp.einsum("qhd,khd->hqk", query_wide, keys_wide) * score_scale
        scores = jnp.where(key_valid[None, None, :], scores, -jnp.inf)
        row_peak = jnp.max(scores, axis=-1, keepdims=True)
        unnormed = jnp.exp(scores - row_peak)
        attention = unnormed / jnp.sum(unnormed, axis=-1, keepdims=True)
        attention_low = narrowed(attention)
        grad_attention = jnp.einsum("qhd,khd->hqk", cotan_wide, values_wide)
        row_total = jnp.sum(attention * grad_attention, axis=-1, keepdims=True)
        grad_scores = narrowed(attention * (grad_attention - row_total) * score_scale)
        query_grad = jnp.einsum("hqk,khd->qhd", grad_scores, keys_wide)
        key_grad = jnp.einsum("hqk,qhd->khd", grad_scores, query_wide).reshape(window_rows, window_cols, features)
        value_grad = jnp.einsum("hqk,qhd->khd", attention_low, cotan_wide).reshape(window_rows, window_cols, features)
        key_patch = lax.dynamic_slice(key_grad_image, starts, sizes) + key_grad
        value_patch = lax.dynamic_slice(value_grad_image, starts, sizes) + value_grad
        key_grad_image = lax.dynamic_update_slice(key_grad_image, key_patch, starts)
        value_grad_image = lax.dynamic_update_slice(value_grad_image, value_patch, starts)
        return (key_grad_image, value_grad_image), query_grad.reshape(TOK_DEV, features).astype(jnp.bfloat16)

    tile_ids = jnp.arange(N_TILE, dtype=jnp.int32)
    images, query_grads = lax.scan(tile_step, (zeros_image, zeros_image), (tile_ids, tiles_query, tiles_cotan))

    def to_tokens(image):
        cropped = image[BAND:BAND + grid_rows * TH, BAND:BAND + TILE_COLS * TW]
        shaped = cropped.reshape(grid_rows, TH, TILE_COLS, TW, features)
        return shaped.transpose(0, 2, 1, 3, 4).reshape(TOKENS, features)

    grad_query = query_grads.reshape(TOKENS, features)
    grad_key = to_tokens(images[0]).astype(jnp.bfloat16)
    grad_value = to_tokens(images[1]).astype(jnp.bfloat16)
    return (grad_query, grad_key, grad_value)
```

```python
import jax
import jax.numpy as jnp
from jax import lax
from jax.experimental import pallas as pl
from jax.experimental.pallas import tpu as pltpu
from jax.sharding import PartitionSpec as P

HD = 128
HEADS_DEV = 3
COLUMNS = 8
ROWS = 16
NY = 8
NX = 4
TOK = 256
STRIP = 64
KEYS = 1024
CHUNK = 128
K_DEV = 768
LOG2E = 1.4426950408889634
SCALE = HD ** (-0.5)
MESH = pl.DeviceIdType.MESH
LAST = (((1,), (1,)), ((), ()))
FIRST = (((0,), (0,)), ((), ()))


def tile_of(x, y, z_hi, core):
    return ((y * 2 + z_hi) * NX + x) * 2 + core


def held_block(y, mp):
    p = lax.rem(y - 2 * mp + 2 * NY, NY)
    upper = (p >= 1) & (p <= 4)
    parity = jnp.where(upper, 1, 0)
    idx = jnp.where(upper, p - 1, lax.rem(NY - p, NY))
    return parity, idx // 2, lax.rem(idx, 2)


def to_halves(tokens):
    wide = tokens.astype(jnp.float32).reshape(16, 2, 8, HD)
    return [wide[:, i].reshape(128, HD).astype(jnp.bfloat16) for i in range(2)]


def kernel(
    q_ref, k_ref, v_ref, g_ref, w_ref, dq_ref, dk_ref, dv_ref,
    win, wpad, stage, wbuf, gpair, part, arrived, bias, prob, grad_s, prob_low, dwin,
    ew_out, ew_in, ns_out, ns_in,
    kvns_s, kvns_r, kvew_s, kvew_r, wsc_s, wsc_r, g_s, g_r, wy_s, wy_r, wx_s, wx_r,
    rs_s, rs_r, dew_s, dew_r, dns_s, dns_r,
):
    t = lax.axis_index("tile")
    mp = lax.axis_index("mp")
    core = lax.rem(t, 2)
    x = lax.rem(t // 2, NX)
    z_hi = lax.rem(t // COLUMNS, 2)
    y = t // (2 * COLUMNS)
    row = t // COLUMNS
    col = lax.rem(t, COLUMNS)
    north = (lax.rem(t + 128 - COLUMNS, 128), mp)
    south = (lax.rem(t + COLUMNS, 128), mp)
    east = (row * COLUMNS + lax.rem(col + 1, COLUMNS), mp)
    west = (row * COLUMNS + lax.rem(col + 7, COLUMNS), mp)
    other = (t + 1 - 2 * core, mp)

    y_par, m_par = lax.rem(y, 2), lax.rem(mp, 2)
    idx = z_hi * 2 + m_par
    p_to = jnp.where(y_par == 1, idx + 1, lax.rem(NY - idx, NY))
    y_to = lax.rem(2 * (y // 2) + p_to, NY)
    scatter_to = [(tile_of(x, y_to, hi, mp // 2), y // 2) for hi in range(2)]
    b_par, b_hi, b_ml = held_block(y, mp)
    scatter_from = [(tile_of(x, 2 * mp + b_par, b_hi, c), 2 * core + b_ml) for c in range(2)]

    def y_peer(d):
        return (tile_of(x, lax.rem(y + d, NY), z_hi, core), mp)

    def x_peer(e):
        return (tile_of(lax.rem(x + e, NX), y, z_hi, core), mp)

    greeted = [north, south, east, west] + scatter_to + scatter_from
    greeted += [y_peer(d) for d in range(1, NY)] + [x_peer(e) for e in range(1, NX)]
    for c in range(2):
        for d in range(4):
            if (c, d) != (0, 0):
                greeted.append((t - core + lax.rem(core + c, 2), lax.rem(mp + d, 4)))
    barrier = pltpu.get_barrier_semaphore()
    for device in greeted:
        pl.semaphore_signal(barrier, inc=1, device_id=device, device_id_type=MESH)

    for h in range(HEADS_DEV):
        lanes = slice(h * HD, (h + 1) * HD)
        for kv, ref in enumerate((k_ref, v_ref)):
            halves = to_halves(ref[:, lanes])
            for i in range(2):
                win[h, kv, 1 + i, STRIP : STRIP + 128, :] = halves[i]
    wpad[0:24, :] = w_ref[...]
    wpad[24:32, :] = jnp.zeros((8, HEADS_DEV * HD), jnp.bfloat16)
    gpair[core] = g_ref[...]
    pl.semaphore_wait(barrier, len(greeted))

    def remote(src, dst, send, recv, device):
        return pltpu.make_async_remote_copy(src, dst, send, recv, device_id=device, device_id_type=MESH)

    sent = []

    def send(src, dst, send_sem, recv_sem, device):
        copy = remote(src, dst, send_sem, recv_sem, device)
        copy.start()
        sent.append(copy)

    def wait_recv(dst, recv_sem):
        remote(dst, dst, recv_sem, recv_sem, other).wait_recv()

    for hi in range(2):
        device = scatter_to[hi]
        mine = (device[0] == t) & (device[1] == mp)
        copy = remote(wpad, stage.at[core], wsc_s.at[hi], wsc_r.at[core], device)
        here = pltpu.make_async_copy(wpad, stage.at[core], wsc_r.at[core])

        @pl.when(mine)
        def _():
            here.start()

        @pl.when(jnp.logical_not(mine))
        def _():
            copy.start()

    def top(h):
        return win.at[h, :, 1:3, STRIP : 2 * STRIP]

    def bottom(h):
        return win.at[h, :, 1:3, 2 * STRIP : 3 * STRIP]

    def halo_n(h):
        return win.at[h, :, 1:3, 0:STRIP]

    def halo_s(h):
        return win.at[h, :, 1:3, 3 * STRIP : 4 * STRIP]

    send(gpair.at[core], gpair.at[core], g_s, g_r, other)
    for h in range(HEADS_DEV):
        send(top(h), halo_s(h), kvns_s.at[h, 0], kvns_r.at[h, 0], north)
        send(bottom(h), halo_n(h), kvns_s.at[h, 1], kvns_r.at[h, 1], south)

    for c in range(2):
        wait_recv(stage.at[c], wsc_r.at[c])

    def block_at(x_at, y_at):
        par, hi, ml = held_block(y_at, mp)
        begin = pl.multiple_of(48 * ((par * 2 + hi) * NX + x_at), 16)
        return wbuf.at[ml, :, pl.ds(begin, 48), :]

    block = stage[:, 0:24, :].astype(jnp.float32).reshape(48, HEADS_DEV * HD).astype(jnp.bfloat16)
    begin = pl.multiple_of(48 * ((b_par * 2 + b_hi) * NX + x), 16)
    for h in range(HEADS_DEV):
        wbuf[b_ml, h, pl.ds(begin, 48), :] = block[:, h * HD : (h + 1) * HD]
    my_block = block_at(x, y)
    y_order = (1, 7, 2, 6, 3, 5, 4)
    x_order = (1, 3, 2)
    for i in range(7):
        d = y_order[i]
        send(my_block, my_block, wy_s.at[d], wy_r.at[d], y_peer(d))
    for e in x_order:
        send(my_block, my_block, wx_s.at[0, e], wx_r.at[0, e], x_peer(e))
    for d in y_order:
        theirs = block_at(x, lax.rem(y + NY - d, NY))
        wait_recv(theirs, wy_r.at[d])
        for e in x_order:
            send(theirs, theirs, wx_s.at[d, e], wx_r.at[d, e], x_peer(e))

    for h in range(HEADS_DEV):
        wait_recv(halo_s(h), kvns_r.at[h, 0])
        wait_recv(halo_n(h), kvns_r.at[h, 1])
        send(win.at[h, :, 1], win.at[h, :, 3], kvew_s.at[h, 0], kvew_r.at[h, 0], west)
        send(win.at[h, :, 2], win.at[h, :, 0], kvew_s.at[h, 1], kvew_r.at[h, 1], east)

    for d in (0,) + y_order:
        for e in x_order:
            theirs = block_at(lax.rem(x + NX - e, NX), lax.rem(y + NY - d, NY))
            wait_recv(theirs, wx_r.at[d, e])
    wait_recv(gpair.at[1 - core], g_r)

    def partial(h):
        weights = jnp.concatenate([wbuf[0, h], wbuf[1, h]], axis=1)
        for c in range(2):
            part[h, c] = jnp.dot(gpair[c], weights, preferred_element_type=jnp.float32).astype(jnp.bfloat16)

    def part_copies(h, ml, c):
        device = (t - core + c, 2 * core + ml)
        mine = (device[0] == t) & (device[1] == mp)
        src = part.at[h, c, :, ml * HD : (ml + 1) * HD]
        dst = arrived.at[h, mp]
        return (
            mine,
            pltpu.make_async_copy(src, dst, rs_r.at[h, mp]),
            remote(src, dst, rs_s.at[h, ml, c], rs_r.at[h, mp], device),
        )

    for h in range(HEADS_DEV):
        partial(h)
        for ml in range(2):
            for c in range(2):
                mine, here, copy = part_copies(h, ml, c)

                @pl.when(mine)
                def _():
                    here.start()

                @pl.when(jnp.logical_not(mine))
                def _():
                    copy.start()

    key_at = lax.broadcasted_iota(jnp.int32, (KEYS, CHUNK), 0)
    group = key_at // 256
    key_row = lax.rem(key_at, 256) // 8
    valid = (
        ((group > 0) | (col > 0))
        & ((group < 3) | (col < COLUMNS - 1))
        & ((key_row >= 8) | (row > 0))
        & ((key_row < 24) | (row < ROWS - 1))
    )
    bias[...] = jnp.where(valid, 0.0, -1e30)
    for h in range(HEADS_DEV):
        wait_recv(win.at[h, :, 3], kvew_r.at[h, 0])
        wait_recv(win.at[h, :, 0], kvew_r.at[h, 1])
        keys = win[h, 0].reshape(KEYS, HD)
        for i in range(2):
            rows = slice(i * CHUNK, (i + 1) * CHUNK)
            scores = lax.dot_general(
                keys, q_ref[rows, h * HD : (h + 1) * HD], LAST, preferred_element_type=jnp.float32
            )
            scores = scores * (SCALE * LOG2E) + bias[...]
            unnormed = jnp.exp2(scores - jnp.max(scores, axis=0, keepdims=True))
            prob[h, i] = unnormed * (1.0 / jnp.sum(unnormed, axis=0, keepdims=True))

    def spread_columns(h):
        send(ew_out.at[h, 0], ew_in.at[h, 0], dew_s.at[h, 0], dew_r.at[h, 0], west)
        send(ew_out.at[h, 1], ew_in.at[h, 1], dew_s.at[h, 1], dew_r.at[h, 1], east)

    def spread_rows(h):
        wait_recv(ew_in.at[h, 0], dew_r.at[h, 0])
        wait_recv(ew_in.at[h, 1], dew_r.at[h, 1])
        for kv in range(2):
            dwin[h, kv, 2] = dwin[h, kv, 2] + ew_in[h, 0, kv].astype(jnp.float32)
            dwin[h, kv, 1] = dwin[h, kv, 1] + ew_in[h, 1, kv].astype(jnp.float32)
            for i in range(2):
                ns_out[h, 0, kv, i] = dwin[h, kv, 1 + i, 0:STRIP].astype(jnp.bfloat16)
                ns_out[h, 1, kv, i] = dwin[h, kv, 1 + i, 3 * STRIP : 4 * STRIP].astype(jnp.bfloat16)
        send(ns_out.at[h, 0], ns_in.at[h, 0], dns_s.at[h, 0], dns_r.at[h, 0], north)
        send(ns_out.at[h, 1], ns_in.at[h, 1], dns_s.at[h, 1], dns_r.at[h, 1], south)

    for h in range(HEADS_DEV):
        lanes = slice(h * HD, (h + 1) * HD)
        total = jnp.zeros((TOK, HD), jnp.float32)
        for s in range(4):
            wait_recv(arrived.at[h, s], rs_r.at[h, s])
            total = total + arrived[h, s].astype(jnp.float32)
        cotangent = total.astype(jnp.bfloat16)
        keys = win[h, 0].reshape(KEYS, HD)
        values = win[h, 1].reshape(KEYS, HD)
        for i in range(2):
            rows = slice(i * CHUNK, (i + 1) * CHUNK)
            attention = prob[h, i]
            grad_attention = lax.dot_general(
                values, cotangent[rows], LAST, preferred_element_type=jnp.float32
            )
            row_total = jnp.sum(attention * grad_attention, axis=0, keepdims=True)
            grad_s[:, rows] = (attention * (grad_attention - row_total) * SCALE).astype(jnp.bfloat16)
            prob_low[:, rows] = attention.astype(jnp.bfloat16)
        dwin[h, 0] = jnp.dot(
            grad_s[...], q_ref[:, lanes], preferred_element_type=jnp.float32
        ).reshape(4, 256, HD)
        dwin[h, 1] = jnp.dot(
            prob_low[...], cotangent, preferred_element_type=jnp.float32
        ).reshape(4, 256, HD)
        for kv in range(2):
            ew_out[h, 0, kv] = dwin[h, kv, 0].astype(jnp.bfloat16)
            ew_out[h, 1, kv] = dwin[h, kv, 3].astype(jnp.bfloat16)
        spread_columns(h)
        dq_ref[:, lanes] = lax.dot_general(
            grad_s[...], keys, FIRST, preferred_element_type=jnp.float32
        ).astype(jnp.bfloat16)
        if h > 0:
            spread_rows(h - 1)
    spread_rows(HEADS_DEV - 1)

    for h in range(HEADS_DEV):
        lanes = slice(h * HD, (h + 1) * HD)
        wait_recv(ns_in.at[h, 0], dns_r.at[h, 0])
        wait_recv(ns_in.at[h, 1], dns_r.at[h, 1])
        for kv, ref in enumerate((dk_ref, dv_ref)):
            halves = []
            for i in range(2):
                upper = dwin[h, kv, 1 + i, STRIP : 2 * STRIP] + ns_in[h, 1, kv, i].astype(jnp.float32)
                lower = dwin[h, kv, 1 + i, 2 * STRIP : 3 * STRIP] + ns_in[h, 0, kv, i].astype(jnp.float32)
                halves.append(jnp.concatenate([upper, lower], axis=0).reshape(16, 8, HD))
            ref[:, lanes] = jnp.stack(halves, axis=1).reshape(TOK, HD).astype(jnp.bfloat16)

    for copy in sent:
        copy.wait_send()
    for hi in range(2):
        device = scatter_to[hi]
        mine = (device[0] == t) & (device[1] == mp)

        @pl.when(jnp.logical_not(mine))
        def _():
            remote(wpad, stage.at[core], wsc_s.at[hi], wsc_r.at[core], device).wait_send()

    for h in range(HEADS_DEV):
        for ml in range(2):
            for c in range(2):
                mine, here, copy = part_copies(h, ml, c)

                @pl.when(jnp.logical_not(mine))
                def _():
                    copy.wait_send()


def shards(query, key, value, grad_y, w_out):
    bf16, f32 = jnp.bfloat16, jnp.float32
    dma = pltpu.SemaphoreType.DMA
    out = jax.ShapeDtypeStruct(query.shape, bf16)
    vmem = pl.BlockSpec(memory_space=pltpu.VMEM)
    return pl.pallas_call(
        kernel,
        name="tiled_attention_backward",
        out_shape=(out, out, out),
        in_specs=[vmem] * 5,
        out_specs=(vmem,) * 3,
        scratch_shapes=[
            pltpu.VMEM((HEADS_DEV, 2, 4, 256, HD), bf16),
            pltpu.VMEM((32, HEADS_DEV * HD), bf16),
            pltpu.VMEM((2, 32, HEADS_DEV * HD), bf16),
            pltpu.VMEM((2, HEADS_DEV, K_DEV, HD), bf16),
            pltpu.VMEM((2, TOK, K_DEV), bf16),
            pltpu.VMEM((HEADS_DEV, 2, TOK, 2 * HD), bf16),
            pltpu.VMEM((HEADS_DEV, 4, TOK, HD), bf16),
            pltpu.VMEM((KEYS, CHUNK), f32),
            pltpu.VMEM((HEADS_DEV, 2, KEYS, CHUNK), f32),
            pltpu.VMEM((KEYS, TOK), bf16),
            pltpu.VMEM((KEYS, TOK), bf16),
            pltpu.VMEM((HEADS_DEV, 2, 4, 256, HD), f32),
            pltpu.VMEM((HEADS_DEV, 2, 2, 256, HD), bf16),
            pltpu.VMEM((HEADS_DEV, 2, 2, 256, HD), bf16),
            pltpu.VMEM((HEADS_DEV, 2, 2, 2, STRIP, HD), bf16),
            pltpu.VMEM((HEADS_DEV, 2, 2, 2, STRIP, HD), bf16),
            dma((HEADS_DEV, 2)), dma((HEADS_DEV, 2)),
            dma((HEADS_DEV, 2)), dma((HEADS_DEV, 2)),
            dma((2,)), dma((2,)),
            dma, dma,
            dma((NY,)), dma((NY,)),
            dma((NY, NX)), dma((NY, NX)),
            dma((HEADS_DEV, 2, 2)), dma((HEADS_DEV, 4)),
            dma((HEADS_DEV, 2)), dma((HEADS_DEV, 2)),
            dma((HEADS_DEV, 2)), dma((HEADS_DEV, 2)),
        ],
        compiler_params=pltpu.CompilerParams(
            collective_id=0, has_side_effects=True, vmem_limit_bytes=48 * 1024 * 1024
        ),
    )(query, key, value, grad_y, w_out)


def solution(mesh):
    spec = P("tile", "mp")
    return jax.shard_map(
        shards, mesh=mesh, in_specs=(spec,) * 5, out_specs=(spec,) * 3, check_vma=False
    )
```

```python
import jax
import jax.numpy as jnp
from jax import lax
from jax.experimental import pallas as pl
from jax.experimental.pallas import tpu as pltpu
from jax.sharding import PartitionSpec as P

HD = 128
HEADS_DEV = 3
COLUMNS = 8
ROWS = 16
NY = 8
NX = 4
TOK = 256
STRIP = 64
KEYS = 1024
CHUNK = 128
K_DEV = 768
K_PAIR = 1536
LOG2E = 1.4426950408889634
SCALE = HD ** (-0.5)
MESH = pl.DeviceIdType.MESH
LAST = (((1,), (1,)), ((), ()))
FIRST = (((0,), (0,)), ((), ()))


def tile_of(x, y, z_hi, core):
    return ((y * 2 + z_hi) * NX + x) * 2 + core


def held_block(y, mp):
    p = lax.rem(y - 4 * (mp // 2) + NY, NY)
    return jnp.where(p < 4, p, 7 - p), jnp.where(p < 4, 0, 1)


def to_halves(tokens):
    wide = tokens.astype(jnp.float32).reshape(16, 2, 8, HD)
    return [wide[:, i].reshape(128, HD).astype(jnp.bfloat16) for i in range(2)]


def kernel(
    q_hbm, k_hbm, v_hbm, g_hbm, w_hbm, dq_ref, dk_ref, dv_ref,
    win, wpad, stage, wbuf, gall, part, arrived, bias, prob, grad_s, prob_low, dwin,
    ew_out, ew_in, ns_out, ns_in, q, k, v, w,
    kvns_s, kvns_r, kvew_s, kvew_r, wsc_s, wsc_r, g_s, g_r, wy_s, wy_r, wx_s, wx_r,
    rs_s, rs_r, dew_s, dew_r, dns_s, dns_r, load,
):
    t = lax.axis_index("tile")
    mp = lax.axis_index("mp")
    core = lax.rem(t, 2)
    x = lax.rem(t // 2, NX)
    z_hi = lax.rem(t // COLUMNS, 2)
    y = t // (2 * COLUMNS)
    row = t // COLUMNS
    col = lax.rem(t, COLUMNS)
    north = (lax.rem(t + 128 - COLUMNS, 128), mp)
    south = (lax.rem(t + COLUMNS, 128), mp)
    east = (row * COLUMNS + lax.rem(col + 1, COLUMNS), mp)
    west = (row * COLUMNS + lax.rem(col + 7, COLUMNS), mp)
    other = (t + 1 - 2 * core, mp)

    half, within = y // 4, lax.rem(y, 4)
    y_to = jnp.where(z_hi == 0, y, lax.rem(4 * half + 7 - within, NY))
    scatter_to = [(tile_of(x, y_to, hi, mp // 2), 2 * half + lax.rem(mp, 2)) for hi in range(2)]
    b_in, b_hi = held_block(y, mp)
    scatter_from = [
        (tile_of(x, 4 * (mp // 2) + b_in, b_hi, c), lax.rem(mp, 2) + 2 * core) for c in range(2)
    ]
    side = lax.rem(mp, 2)
    pair = mp + 1 - 2 * side
    far = lax.rem(mp + 2, 4)
    block_of_heads = side + 2 * core

    def y_peer(d):
        return (tile_of(x, lax.rem(y + d, NY), z_hi, core), mp)

    def x_peer(e):
        return (tile_of(lax.rem(x + e, NX), y, z_hi, core), mp)

    greeted = [north, south, east, west] + scatter_to + scatter_from
    greeted += [y_peer(d) for d in range(1, NY)] + [x_peer(e) for e in range(1, NX)]
    greeted += [(t, pair), (t, far), (other[0], far)]
    barrier = pltpu.get_barrier_semaphore()
    for device in greeted:
        pl.semaphore_signal(barrier, inc=1, device_id=device, device_id_type=MESH)

    loads = []
    for i, (src, dst) in enumerate(
        ((w_hbm, w), (k_hbm, k), (v_hbm, v), (g_hbm, gall.at[side, core]), (q_hbm, q))
    ):
        loads.append(pltpu.make_async_copy(src, dst, load.at[i]))
        loads[-1].start()

    loads[0].wait()
    wpad[0:24, :] = w[...]
    wpad[24:32, :] = jnp.zeros((8, HEADS_DEV * HD), jnp.bfloat16)
    loads[1].wait()
    loads[2].wait()
    for h in range(HEADS_DEV):
        lanes = slice(h * HD, (h + 1) * HD)
        for kv, ref in enumerate((k, v)):
            halves = to_halves(ref[:, lanes])
            for i in range(2):
                win[h, kv, 1 + i, STRIP : STRIP + 128, :] = halves[i]
    loads[3].wait()
    pl.semaphore_wait(barrier, len(greeted))

    def remote(src, dst, send, recv, device):
        return pltpu.make_async_remote_copy(src, dst, send, recv, device_id=device, device_id_type=MESH)

    sent = []

    def send(src, dst, send_sem, recv_sem, device):
        copy = remote(src, dst, send_sem, recv_sem, device)
        copy.start()
        sent.append(copy)

    def wait_recv(dst, recv_sem):
        remote(dst, dst, recv_sem, recv_sem, other).wait_recv()

    for hi in range(2):
        device = scatter_to[hi]
        mine = (device[0] == t) & (device[1] == mp)

        @pl.when(mine)
        def _():
            pltpu.make_async_copy(wpad, stage.at[core], wsc_r.at[core]).start()

        @pl.when(jnp.logical_not(mine))
        def _():
            remote(wpad, stage.at[core], wsc_s.at[hi], wsc_r.at[core], device).start()

    def top(h):
        return win.at[h, :, 1:3, STRIP : 2 * STRIP]

    def bottom(h):
        return win.at[h, :, 1:3, 2 * STRIP : 3 * STRIP]

    def halo_n(h):
        return win.at[h, :, 1:3, 0:STRIP]

    def halo_s(h):
        return win.at[h, :, 1:3, 3 * STRIP : 4 * STRIP]

    mine_g = gall.at[side, core]
    near_g = gall.at[1 - side, core]
    send(mine_g, mine_g, g_s.at[0], g_r.at[0], (t, pair))
    send(mine_g, mine_g, g_s.at[1], g_r.at[1], other)
    for h in range(HEADS_DEV):
        send(top(h), halo_s(h), kvns_s.at[h, 0], kvns_r.at[h, 0], north)
        send(bottom(h), halo_n(h), kvns_s.at[h, 1], kvns_r.at[h, 1], south)

    for c in range(2):
        wait_recv(stage.at[c], wsc_r.at[c])

    def block_at(x_at, y_at):
        inside, hi = held_block(y_at, mp)
        begin = pl.multiple_of(48 * ((inside * 2 + hi) * NX + x_at), 16)
        return wbuf.at[:, pl.ds(begin, 48), :]

    block = stage[:, 0:24, :].astype(jnp.float32).reshape(48, HEADS_DEV * HD).astype(jnp.bfloat16)
    begin = pl.multiple_of(48 * ((b_in * 2 + b_hi) * NX + x), 16)
    for h in range(HEADS_DEV):
        wbuf[h, pl.ds(begin, 48), :] = block[:, h * HD : (h + 1) * HD]
    my_block = block_at(x, y)
    y_order = (1, 7, 2, 6, 3, 5, 4)
    x_order = (1, 3, 2)
    for d in y_order:
        send(my_block, my_block, wy_s.at[d], wy_r.at[d], y_peer(d))
    for e in x_order:
        send(my_block, my_block, wx_s.at[0, e], wx_r.at[0, e], x_peer(e))
    for d in y_order:
        theirs = block_at(x, lax.rem(y + NY - d, NY))
        wait_recv(theirs, wy_r.at[d])
        for e in x_order:
            send(theirs, theirs, wx_s.at[d, e], wx_r.at[d, e], x_peer(e))

    wait_recv(near_g, g_r.at[0])
    send(near_g, near_g, g_s.at[2], g_r.at[2], other)
    wait_recv(gall.at[side, 1 - core], g_r.at[1])
    wait_recv(gall.at[1 - side, 1 - core], g_r.at[2])

    for d in (0,) + y_order:
        for e in x_order:
            theirs = block_at(lax.rem(x + NX - e, NX), lax.rem(y + NY - d, NY))
            wait_recv(theirs, wx_r.at[d, e])

    slot = jnp.where(block_of_heads == mp, 0, 1)

    def part_copy(h, c):
        device = (t - core + c, block_of_heads)
        mine = (block_of_heads == mp) & (core == c)
        return mine, remote(part.at[h, c], arrived.at[h, slot], rs_s.at[h, c], rs_r.at[h, slot], device)

    for h in range(HEADS_DEV):
        total = jnp.zeros((2 * TOK, HD), jnp.float32)
        for i in range(2):
            total = total + jnp.dot(
                gall[i].reshape(2 * TOK, K_DEV),
                wbuf[h, i * K_DEV : (i + 1) * K_DEV, :],
                preferred_element_type=jnp.float32,
            )
        part[h] = total.reshape(2, TOK, HD).astype(jnp.bfloat16)
        for c in range(2):
            mine, copy = part_copy(h, c)

            @pl.when(mine)
            def _():
                pltpu.make_async_copy(part.at[h, c], arrived.at[h, slot], rs_r.at[h, slot]).start()

            @pl.when(jnp.logical_not(mine))
            def _():
                copy.start()

    for h in range(HEADS_DEV):
        wait_recv(halo_s(h), kvns_r.at[h, 0])
        wait_recv(halo_n(h), kvns_r.at[h, 1])
        send(win.at[h, :, 1], win.at[h, :, 3], kvew_s.at[h, 0], kvew_r.at[h, 0], west)
        send(win.at[h, :, 2], win.at[h, :, 0], kvew_s.at[h, 1], kvew_r.at[h, 1], east)

    loads[4].wait()
    key_at = lax.broadcasted_iota(jnp.int32, (KEYS, CHUNK), 0)
    group = key_at // 256
    key_row = lax.rem(key_at, 256) // 8
    valid = (
        ((group > 0) | (col > 0))
        & ((group < 3) | (col < COLUMNS - 1))
        & ((key_row >= 8) | (row > 0))
        & ((key_row < 24) | (row < ROWS - 1))
    )
    bias[...] = jnp.where(valid, 0.0, -1e30)
    for h in range(HEADS_DEV):
        wait_recv(win.at[h, :, 3], kvew_r.at[h, 0])
        wait_recv(win.at[h, :, 0], kvew_r.at[h, 1])
        keys = win[h, 0].reshape(KEYS, HD)
        for i in range(2):
            rows = slice(i * CHUNK, (i + 1) * CHUNK)
            scores = lax.dot_general(
                keys, q[rows, h * HD : (h + 1) * HD], LAST, preferred_element_type=jnp.float32
            )
            scores = scores * (SCALE * LOG2E) + bias[...]
            unnormed = jnp.exp2(scores - jnp.max(scores, axis=0, keepdims=True))
            prob[h, i] = unnormed * (1.0 / jnp.sum(unnormed, axis=0, keepdims=True))

    def spread_columns(h):
        send(ew_out.at[h, 0], ew_in.at[h, 0], dew_s.at[h, 0], dew_r.at[h, 0], west)
        send(ew_out.at[h, 1], ew_in.at[h, 1], dew_s.at[h, 1], dew_r.at[h, 1], east)

    def spread_rows(h):
        wait_recv(ew_in.at[h, 0], dew_r.at[h, 0])
        wait_recv(ew_in.at[h, 1], dew_r.at[h, 1])
        for kv in range(2):
            dwin[h, kv, 2] = dwin[h, kv, 2] + ew_in[h, 0, kv].astype(jnp.float32)
            dwin[h, kv, 1] = dwin[h, kv, 1] + ew_in[h, 1, kv].astype(jnp.float32)
            for i in range(2):
                ns_out[h, 0, kv, i] = dwin[h, kv, 1 + i, 0:STRIP].astype(jnp.bfloat16)
                ns_out[h, 1, kv, i] = dwin[h, kv, 1 + i, 3 * STRIP : 4 * STRIP].astype(jnp.bfloat16)
        send(ns_out.at[h, 0], ns_in.at[h, 0], dns_s.at[h, 0], dns_r.at[h, 0], north)
        send(ns_out.at[h, 1], ns_in.at[h, 1], dns_s.at[h, 1], dns_r.at[h, 1], south)

    for h in range(HEADS_DEV):
        lanes = slice(h * HD, (h + 1) * HD)
        total = jnp.zeros((TOK, HD), jnp.float32)
        for s in range(2):
            wait_recv(arrived.at[h, s], rs_r.at[h, s])
            total = total + arrived[h, s].astype(jnp.float32)
        cotangent = total.astype(jnp.bfloat16)
        keys = win[h, 0].reshape(KEYS, HD)
        values = win[h, 1].reshape(KEYS, HD)
        for i in range(2):
            rows = slice(i * CHUNK, (i + 1) * CHUNK)
            attention = prob[h, i]
            grad_attention = lax.dot_general(
                values, cotangent[rows], LAST, preferred_element_type=jnp.float32
            )
            row_total = jnp.sum(attention * grad_attention, axis=0, keepdims=True)
            grad_s[:, rows] = (attention * (grad_attention - row_total) * SCALE).astype(jnp.bfloat16)
            prob_low[:, rows] = attention.astype(jnp.bfloat16)
        dwin[h, 0] = jnp.dot(
            grad_s[...], q[:, lanes], preferred_element_type=jnp.float32
        ).reshape(4, 256, HD)
        dwin[h, 1] = jnp.dot(
            prob_low[...], cotangent, preferred_element_type=jnp.float32
        ).reshape(4, 256, HD)
        for kv in range(2):
            ew_out[h, 0, kv] = dwin[h, kv, 0].astype(jnp.bfloat16)
            ew_out[h, 1, kv] = dwin[h, kv, 3].astype(jnp.bfloat16)
        spread_columns(h)
        dq_ref[:, lanes] = lax.dot_general(
            grad_s[...], keys, FIRST, preferred_element_type=jnp.float32
        ).astype(jnp.bfloat16)
        if h > 0:
            spread_rows(h - 1)
    spread_rows(HEADS_DEV - 1)

    for h in range(HEADS_DEV):
        lanes = slice(h * HD, (h + 1) * HD)
        wait_recv(ns_in.at[h, 0], dns_r.at[h, 0])
        wait_recv(ns_in.at[h, 1], dns_r.at[h, 1])
        for kv, ref in enumerate((dk_ref, dv_ref)):
            halves = []
            for i in range(2):
                upper = dwin[h, kv, 1 + i, STRIP : 2 * STRIP] + ns_in[h, 1, kv, i].astype(jnp.float32)
                lower = dwin[h, kv, 1 + i, 2 * STRIP : 3 * STRIP] + ns_in[h, 0, kv, i].astype(jnp.float32)
                halves.append(jnp.concatenate([upper, lower], axis=0).reshape(16, 8, HD))
            ref[:, lanes] = jnp.stack(halves, axis=1).reshape(TOK, HD).astype(jnp.bfloat16)

    for copy in sent:
        copy.wait_send()
    for hi in range(2):
        device = scatter_to[hi]
        mine = (device[0] == t) & (device[1] == mp)

        @pl.when(jnp.logical_not(mine))
        def _():
            remote(wpad, stage.at[core], wsc_s.at[hi], wsc_r.at[core], device).wait_send()

    for h in range(HEADS_DEV):
        for c in range(2):
            mine, copy = part_copy(h, c)

            @pl.when(jnp.logical_not(mine))
            def _():
                copy.wait_send()


def shards(query, key, value, grad_y, w_out):
    bf16, f32 = jnp.bfloat16, jnp.float32
    dma = pltpu.SemaphoreType.DMA
    out = jax.ShapeDtypeStruct(query.shape, bf16)
    vmem = pl.BlockSpec(memory_space=pltpu.VMEM)
    hbm = pl.BlockSpec(memory_space=pltpu.HBM)
    return pl.pallas_call(
        kernel,
        name="tiled_attention_backward",
        out_shape=(out, out, out),
        in_specs=[hbm] * 5,
        out_specs=(vmem,) * 3,
        scratch_shapes=[
            pltpu.VMEM((HEADS_DEV, 2, 4, 256, HD), bf16),
            pltpu.VMEM((32, HEADS_DEV * HD), bf16),
            pltpu.VMEM((2, 32, HEADS_DEV * HD), bf16),
            pltpu.VMEM((HEADS_DEV, K_PAIR, HD), bf16),
            pltpu.VMEM((2, 2, TOK, K_DEV), bf16),
            pltpu.VMEM((HEADS_DEV, 2, TOK, HD), bf16),
            pltpu.VMEM((HEADS_DEV, 2, TOK, HD), bf16),
            pltpu.VMEM((KEYS, CHUNK), f32),
            pltpu.VMEM((HEADS_DEV, 2, KEYS, CHUNK), f32),
            pltpu.VMEM((KEYS, TOK), bf16),
            pltpu.VMEM((KEYS, TOK), bf16),
            pltpu.VMEM((HEADS_DEV, 2, 4, 256, HD), f32),
            pltpu.VMEM((HEADS_DEV, 2, 2, 256, HD), bf16),
            pltpu.VMEM((HEADS_DEV, 2, 2, 256, HD), bf16),
            pltpu.VMEM((HEADS_DEV, 2, 2, 2, STRIP, HD), bf16),
            pltpu.VMEM((HEADS_DEV, 2, 2, 2, STRIP, HD), bf16),
            pltpu.VMEM(query.shape, bf16),
            pltpu.VMEM(key.shape, bf16),
            pltpu.VMEM(value.shape, bf16),
            pltpu.VMEM(w_out.shape, bf16),
            dma((HEADS_DEV, 2)), dma((HEADS_DEV, 2)),
            dma((HEADS_DEV, 2)), dma((HEADS_DEV, 2)),
            dma((2,)), dma((2,)),
            dma((3,)), dma((3,)),
            dma((NY,)), dma((NY,)),
            dma((NY, NX)), dma((NY, NX)),
            dma((HEADS_DEV, 2)), dma((HEADS_DEV, 2)),
            dma((HEADS_DEV, 2)), dma((HEADS_DEV, 2)),
            dma((HEADS_DEV, 2)), dma((HEADS_DEV, 2)),
            dma((5,)),
        ],
        compiler_params=pltpu.CompilerParams(
            collective_id=0, has_side_effects=True, vmem_limit_bytes=48 * 1024 * 1024
        ),
    )(query, key, value, grad_y, w_out)


def solution(mesh):
    spec = P("tile", "mp")
    return jax.shard_map(
        shards, mesh=mesh, in_specs=(spec,) * 5, out_specs=(spec,) * 3, check_vma=False
    )
```

```python
import jax
import jax.numpy as jnp
from jax import lax
from jax.experimental import pallas as pl
from jax.experimental.pallas import tpu as pltpu
from jax.sharding import PartitionSpec as P

HD = 128
HEADS_DEV = 3
COLUMNS = 8
ROWS = 16
NY = 8
NX = 4
TOK = 256
STRIP = 64
KEYS = 1024
CHUNK = 128
K_DEV = 768
K_PAIR = 1536
LOG2E = 1.4426950408889634
SCALE = HD ** (-0.5)
MESH = pl.DeviceIdType.MESH
LAST = (((1,), (1,)), ((), ()))
FIRST = (((0,), (0,)), ((), ()))


def tile_of(x, y, z_hi, core):
    return ((y * 2 + z_hi) * NX + x) * 2 + core


def held_block(y, mp):
    p = lax.rem(y - 4 * (mp // 2) + NY, NY)
    return jnp.where(p < 4, p, 7 - p), jnp.where(p < 4, 0, 1)


def to_halves(tokens):
    wide = tokens.astype(jnp.float32).reshape(16, 2, 8, HD)
    return [wide[:, i].reshape(128, HD).astype(jnp.bfloat16) for i in range(2)]


def kernel(
    q_hbm, k_hbm, v_hbm, g_hbm, w_hbm, dq_ref, dk_ref, dv_ref,
    win, wpad, stage, wbuf, gall, part, arrived, bias, prob, grad_s, prob_low, dwin,
    ew_out, ew_in, ns_out, ns_in, q, k, v, w,
    kvns_s, kvns_r, kvew_s, kvew_r, wsc_s, wsc_r, g_s, g_r, wy_s, wy_r, wx_s, wx_r,
    rs_s, rs_r, dew_s, dew_r, dns_s, dns_r, load,
):
    t = lax.axis_index("tile")
    mp = lax.axis_index("mp")
    core = lax.rem(t, 2)
    x = lax.rem(t // 2, NX)
    z_hi = lax.rem(t // COLUMNS, 2)
    y = t // (2 * COLUMNS)
    row = t // COLUMNS
    col = lax.rem(t, COLUMNS)
    north = (lax.rem(t + 128 - COLUMNS, 128), mp)
    south = (lax.rem(t + COLUMNS, 128), mp)
    east = (row * COLUMNS + lax.rem(col + 1, COLUMNS), mp)
    west = (row * COLUMNS + lax.rem(col + 7, COLUMNS), mp)
    other = (t + 1 - 2 * core, mp)

    half, within = y // 4, lax.rem(y, 4)
    y_to = jnp.where(z_hi == 0, y, lax.rem(4 * half + 7 - within, NY))
    scatter_to = [(tile_of(x, y_to, hi, mp // 2), 2 * half + lax.rem(mp, 2)) for hi in range(2)]
    b_in, b_hi = held_block(y, mp)
    scatter_from = [
        (tile_of(x, 4 * (mp // 2) + b_in, b_hi, c), lax.rem(mp, 2) + 2 * core) for c in range(2)
    ]
    side = lax.rem(mp, 2)
    pair = mp + 1 - 2 * side
    far = lax.rem(mp + 2, 4)
    block_of_heads = side + 2 * core

    def y_peer(d):
        return (tile_of(x, lax.rem(y + d, NY), z_hi, core), mp)

    def x_peer(e):
        return (tile_of(lax.rem(x + e, NX), y, z_hi, core), mp)

    greeted = [north, south, east, west] + scatter_to + scatter_from
    greeted += [y_peer(d) for d in range(1, NY)] + [x_peer(e) for e in range(1, NX)]
    greeted += [(t, pair), (t, far), (other[0], far)]
    barrier = pltpu.get_barrier_semaphore()
    for device in greeted:
        pl.semaphore_signal(barrier, inc=1, device_id=device, device_id_type=MESH)

    loads = []
    for i, (src, dst) in enumerate(
        ((w_hbm, w), (k_hbm, k), (v_hbm, v), (g_hbm, gall.at[side, core]), (q_hbm, q))
    ):
        loads.append(pltpu.make_async_copy(src, dst, load.at[i]))
        loads[-1].start()

    loads[0].wait()
    wpad[0:24, :] = w[...]
    wpad[24:32, :] = jnp.zeros((8, HEADS_DEV * HD), jnp.bfloat16)
    loads[1].wait()
    loads[2].wait()
    for h in range(HEADS_DEV):
        lanes = slice(h * HD, (h + 1) * HD)
        for kv, ref in enumerate((k, v)):
            halves = to_halves(ref[:, lanes])
            for i in range(2):
                win[h, kv, 1 + i, STRIP : STRIP + 128, :] = halves[i]
    loads[3].wait()
    pl.semaphore_wait(barrier, len(greeted))

    def remote(src, dst, send, recv, device):
        return pltpu.make_async_remote_copy(src, dst, send, recv, device_id=device, device_id_type=MESH)

    sent = []

    def send(src, dst, send_sem, recv_sem, device):
        copy = remote(src, dst, send_sem, recv_sem, device)
        copy.start()
        sent.append(copy)

    def wait_recv(dst, recv_sem):
        remote(dst, dst, recv_sem, recv_sem, other).wait_recv()

    for hi in range(2):
        device = scatter_to[hi]
        mine = (device[0] == t) & (device[1] == mp)

        @pl.when(mine)
        def _():
            pltpu.make_async_copy(wpad, stage.at[core], wsc_r.at[core]).start()

        @pl.when(jnp.logical_not(mine))
        def _():
            remote(wpad, stage.at[core], wsc_s.at[hi], wsc_r.at[core], device).start()

    def top(h):
        return win.at[h, :, 1:3, STRIP : 2 * STRIP]

    def bottom(h):
        return win.at[h, :, 1:3, 2 * STRIP : 3 * STRIP]

    def halo_n(h):
        return win.at[h, :, 1:3, 0:STRIP]

    def halo_s(h):
        return win.at[h, :, 1:3, 3 * STRIP : 4 * STRIP]

    mine_g = gall.at[side, core]
    near_g = gall.at[1 - side, core]
    send(mine_g, mine_g, g_s.at[0], g_r.at[0], (t, pair))
    send(mine_g, mine_g, g_s.at[1], g_r.at[1], other)

    def halo_rows(h):
        send(top(h), halo_s(h), kvns_s.at[h, 0], kvns_r.at[h, 0], north)
        send(bottom(h), halo_n(h), kvns_s.at[h, 1], kvns_r.at[h, 1], south)

    def halo_columns(h):
        wait_recv(halo_s(h), kvns_r.at[h, 0])
        wait_recv(halo_n(h), kvns_r.at[h, 1])
        send(win.at[h, :, 1], win.at[h, :, 3], kvew_s.at[h, 0], kvew_r.at[h, 0], west)
        send(win.at[h, :, 2], win.at[h, :, 0], kvew_s.at[h, 1], kvew_r.at[h, 1], east)

    halo_rows(0)
    halo_rows(1)
    halo_rows(2)

    for c in range(2):
        wait_recv(stage.at[c], wsc_r.at[c])

    def block_at(x_at, y_at):
        inside, hi = held_block(y_at, mp)
        begin = pl.multiple_of(48 * ((inside * 2 + hi) * NX + x_at), 16)
        return wbuf.at[:, pl.ds(begin, 48), :]

    block = stage[:, 0:24, :].astype(jnp.float32).reshape(48, HEADS_DEV * HD).astype(jnp.bfloat16)
    begin = pl.multiple_of(48 * ((b_in * 2 + b_hi) * NX + x), 16)
    for h in range(HEADS_DEV):
        wbuf[h, pl.ds(begin, 48), :] = block[:, h * HD : (h + 1) * HD]
    my_block = block_at(x, y)
    y_order = (1, 7, 2, 6, 3, 5, 4)
    x_order = (1, 3, 2)
    for d in y_order:
        send(my_block, my_block, wy_s.at[d], wy_r.at[d], y_peer(d))
    for e in x_order:
        send(my_block, my_block, wx_s.at[0, e], wx_r.at[0, e], x_peer(e))
    for d in y_order:
        theirs = block_at(x, lax.rem(y + NY - d, NY))
        wait_recv(theirs, wy_r.at[d])
        for e in x_order:
            send(theirs, theirs, wx_s.at[d, e], wx_r.at[d, e], x_peer(e))

    wait_recv(near_g, g_r.at[0])
    send(near_g, near_g, g_s.at[2], g_r.at[2], other)
    wait_recv(gall.at[side, 1 - core], g_r.at[1])
    wait_recv(gall.at[1 - side, 1 - core], g_r.at[2])

    for d in (0,) + y_order:
        for e in x_order:
            theirs = block_at(lax.rem(x + NX - e, NX), lax.rem(y + NY - d, NY))
            wait_recv(theirs, wx_r.at[d, e])

    slot = jnp.where(block_of_heads == mp, 0, 1)

    def part_copy(h, c):
        device = (t - core + c, block_of_heads)
        mine = (block_of_heads == mp) & (core == c)
        return mine, remote(part.at[h, c], arrived.at[h, slot], rs_s.at[h, c], rs_r.at[h, slot], device)

    def share(h):
        total = jnp.zeros((2 * TOK, HD), jnp.float32)
        for i in range(2):
            total = total + jnp.dot(
                gall[i].reshape(2 * TOK, K_DEV),
                wbuf[h, i * K_DEV : (i + 1) * K_DEV, :],
                preferred_element_type=jnp.float32,
            )
        part[h] = total.reshape(2, TOK, HD).astype(jnp.bfloat16)
        for c in range(2):
            mine, copy = part_copy(h, c)

            @pl.when(mine)
            def _():
                pltpu.make_async_copy(part.at[h, c], arrived.at[h, slot], rs_r.at[h, slot]).start()

            @pl.when(jnp.logical_not(mine))
            def _():
                copy.start()

    share(0)
    share(1)
    share(2)

    halo_columns(0)
    halo_columns(1)
    halo_columns(2)
    loads[4].wait()
    key_at = lax.broadcasted_iota(jnp.int32, (KEYS, CHUNK), 0)
    group = key_at // 256
    key_row = lax.rem(key_at, 256) // 8
    valid = (
        ((group > 0) | (col > 0))
        & ((group < 3) | (col < COLUMNS - 1))
        & ((key_row >= 8) | (row > 0))
        & ((key_row < 24) | (row < ROWS - 1))
    )
    bias[...] = jnp.where(valid, 0.0, -1e30)

    def softmax(h):
        wait_recv(win.at[h, :, 3], kvew_r.at[h, 0])
        wait_recv(win.at[h, :, 0], kvew_r.at[h, 1])
        keys = win[h, 0].reshape(KEYS, HD)
        for i in range(2):
            rows = slice(i * CHUNK, (i + 1) * CHUNK)
            scores = lax.dot_general(
                keys, q[rows, h * HD : (h + 1) * HD], LAST, preferred_element_type=jnp.float32
            )
            scores = scores * (SCALE * LOG2E) + bias[...]
            unnormed = jnp.exp2(scores - jnp.max(scores, axis=0, keepdims=True))
            prob[h, i] = unnormed * (1.0 / jnp.sum(unnormed, axis=0, keepdims=True))

    def spread_columns(h):
        send(ew_out.at[h, 0], ew_in.at[h, 0], dew_s.at[h, 0], dew_r.at[h, 0], west)
        send(ew_out.at[h, 1], ew_in.at[h, 1], dew_s.at[h, 1], dew_r.at[h, 1], east)

    def spread_rows(h):
        wait_recv(ew_in.at[h, 0], dew_r.at[h, 0])
        wait_recv(ew_in.at[h, 1], dew_r.at[h, 1])
        for kv in range(2):
            dwin[h, kv, 2] = dwin[h, kv, 2] + ew_in[h, 0, kv].astype(jnp.float32)
            dwin[h, kv, 1] = dwin[h, kv, 1] + ew_in[h, 1, kv].astype(jnp.float32)
            for i in range(2):
                ns_out[h, 0, kv, i] = dwin[h, kv, 1 + i, 0:STRIP].astype(jnp.bfloat16)
                ns_out[h, 1, kv, i] = dwin[h, kv, 1 + i, 3 * STRIP : 4 * STRIP].astype(jnp.bfloat16)
        send(ns_out.at[h, 0], ns_in.at[h, 0], dns_s.at[h, 0], dns_r.at[h, 0], north)
        send(ns_out.at[h, 1], ns_in.at[h, 1], dns_s.at[h, 1], dns_r.at[h, 1], south)

    def backward(h):
        lanes = slice(h * HD, (h + 1) * HD)
        total = jnp.zeros((TOK, HD), jnp.float32)
        for s in range(2):
            wait_recv(arrived.at[h, s], rs_r.at[h, s])
            total = total + arrived[h, s].astype(jnp.float32)
        cotangent = total.astype(jnp.bfloat16)
        keys = win[h, 0].reshape(KEYS, HD)
        values = win[h, 1].reshape(KEYS, HD)
        for i in range(2):
            rows = slice(i * CHUNK, (i + 1) * CHUNK)
            attention = prob[h, i]
            grad_attention = lax.dot_general(
                values, cotangent[rows], LAST, preferred_element_type=jnp.float32
            )
            row_total = jnp.sum(attention * grad_attention, axis=0, keepdims=True)
            grad_s[:, rows] = (attention * (grad_attention - row_total) * SCALE).astype(jnp.bfloat16)
            prob_low[:, rows] = attention.astype(jnp.bfloat16)
        dwin[h, 0] = jnp.dot(
            grad_s[...], q[:, lanes], preferred_element_type=jnp.float32
        ).reshape(4, 256, HD)
        dwin[h, 1] = jnp.dot(
            prob_low[...], cotangent, preferred_element_type=jnp.float32
        ).reshape(4, 256, HD)
        for kv in range(2):
            ew_out[h, 0, kv] = dwin[h, kv, 0].astype(jnp.bfloat16)
            ew_out[h, 1, kv] = dwin[h, kv, 3].astype(jnp.bfloat16)
        spread_columns(h)
        dq_ref[:, lanes] = lax.dot_general(
            grad_s[...], keys, FIRST, preferred_element_type=jnp.float32
        ).astype(jnp.bfloat16)

    def finish(h):
        lanes = slice(h * HD, (h + 1) * HD)
        wait_recv(ns_in.at[h, 0], dns_r.at[h, 0])
        wait_recv(ns_in.at[h, 1], dns_r.at[h, 1])
        for kv, ref in enumerate((dk_ref, dv_ref)):
            halves = []
            for i in range(2):
                upper = dwin[h, kv, 1 + i, STRIP : 2 * STRIP] + ns_in[h, 1, kv, i].astype(jnp.float32)
                lower = dwin[h, kv, 1 + i, 2 * STRIP : 3 * STRIP] + ns_in[h, 0, kv, i].astype(jnp.float32)
                halves.append(jnp.concatenate([upper, lower], axis=0).reshape(16, 8, HD))
            ref[:, lanes] = jnp.stack(halves, axis=1).reshape(TOK, HD).astype(jnp.bfloat16)

    softmax(0)
    backward(0)
    softmax(1)
    spread_rows(0)
    backward(1)
    softmax(2)
    spread_rows(1)
    backward(2)
    spread_rows(2)
    for h in range(HEADS_DEV):
        finish(h)

    for copy in sent:
        copy.wait_send()
    for hi in range(2):
        device = scatter_to[hi]
        mine = (device[0] == t) & (device[1] == mp)

        @pl.when(jnp.logical_not(mine))
        def _():
            remote(wpad, stage.at[core], wsc_s.at[hi], wsc_r.at[core], device).wait_send()

    for h in range(HEADS_DEV):
        for c in range(2):
            mine, copy = part_copy(h, c)

            @pl.when(jnp.logical_not(mine))
            def _():
                copy.wait_send()


def shards(query, key, value, grad_y, w_out):
    bf16, f32 = jnp.bfloat16, jnp.float32
    dma = pltpu.SemaphoreType.DMA
    out = jax.ShapeDtypeStruct(query.shape, bf16)
    vmem = pl.BlockSpec(memory_space=pltpu.VMEM)
    hbm = pl.BlockSpec(memory_space=pltpu.HBM)
    return pl.pallas_call(
        kernel,
        name="tiled_attention_backward",
        out_shape=(out, out, out),
        in_specs=[hbm] * 5,
        out_specs=(vmem,) * 3,
        scratch_shapes=[
            pltpu.VMEM((HEADS_DEV, 2, 4, 256, HD), bf16),
            pltpu.VMEM((32, HEADS_DEV * HD), bf16),
            pltpu.VMEM((2, 32, HEADS_DEV * HD), bf16),
            pltpu.VMEM((HEADS_DEV, K_PAIR, HD), bf16),
            pltpu.VMEM((2, 2, TOK, K_DEV), bf16),
            pltpu.VMEM((HEADS_DEV, 2, TOK, HD), bf16),
            pltpu.VMEM((HEADS_DEV, 2, TOK, HD), bf16),
            pltpu.VMEM((KEYS, CHUNK), f32),
            pltpu.VMEM((HEADS_DEV, 2, KEYS, CHUNK), f32),
            pltpu.VMEM((KEYS, TOK), bf16),
            pltpu.VMEM((KEYS, TOK), bf16),
            pltpu.VMEM((HEADS_DEV, 2, 4, 256, HD), f32),
            pltpu.VMEM((HEADS_DEV, 2, 2, 256, HD), bf16),
            pltpu.VMEM((HEADS_DEV, 2, 2, 256, HD), bf16),
            pltpu.VMEM((HEADS_DEV, 2, 2, 2, STRIP, HD), bf16),
            pltpu.VMEM((HEADS_DEV, 2, 2, 2, STRIP, HD), bf16),
            pltpu.VMEM(query.shape, bf16),
            pltpu.VMEM(key.shape, bf16),
            pltpu.VMEM(value.shape, bf16),
            pltpu.VMEM(w_out.shape, bf16),
            dma((HEADS_DEV, 2)), dma((HEADS_DEV, 2)),
            dma((HEADS_DEV, 2)), dma((HEADS_DEV, 2)),
            dma((2,)), dma((2,)),
            dma((3,)), dma((3,)),
            dma((NY,)), dma((NY,)),
            dma((NY, NX)), dma((NY, NX)),
            dma((HEADS_DEV, 2)), dma((HEADS_DEV, 2)),
            dma((HEADS_DEV, 2)), dma((HEADS_DEV, 2)),
            dma((HEADS_DEV, 2)), dma((HEADS_DEV, 2)),
            dma((5,)),
        ],
        compiler_params=pltpu.CompilerParams(
            collective_id=0, has_side_effects=True, vmem_limit_bytes=60 * 1024 * 1024
        ),
    )(query, key, value, grad_y, w_out)


def solution(mesh):
    spec = P("tile", "mp")
    return jax.shard_map(
        shards, mesh=mesh, in_specs=(spec,) * 5, out_specs=(spec,) * 3, check_vma=False
    )
```

```python
import jax
import jax.numpy as jnp
from jax import lax
from jax.experimental import pallas as pl
from jax.experimental.pallas import tpu as pltpu
from jax.sharding import PartitionSpec as P

HD = 128
HEADS_DEV = 3
COLUMNS = 8
ROWS = 16
NY = 8
NX = 4
TOK = 256
STRIP = 64
KEYS = 1024
CHUNK = 128
K_DEV = 768
K_PAIR = 1536
LOG2E = 1.4426950408889634
SCALE = HD ** (-0.5)
MESH = pl.DeviceIdType.MESH
LAST = (((1,), (1,)), ((), ()))
FIRST = (((0,), (0,)), ((), ()))


def tile_of(x, y, z_hi, core):
    return ((y * 2 + z_hi) * NX + x) * 2 + core


def held_block(y, mp):
    p = lax.rem(y - 4 * (mp // 2) + NY, NY)
    return jnp.where(p < 4, p, 7 - p), jnp.where(p < 4, 0, 1)


def to_halves(tokens):
    wide = tokens.astype(jnp.float32).reshape(16, 2, 8, HD)
    return [wide[:, i].reshape(128, HD).astype(jnp.bfloat16) for i in range(2)]


def kernel(
    q_hbm, k_hbm, v_hbm, g_hbm, w_hbm, dq_hbm, dk_hbm, dv_hbm,
    win, wpad, stage, wbuf, gall, part, arrived, bias, prob, grad_s, prob_low, dwin,
    ew_out, ew_in, ns_out, ns_in, q, k, v, w, out,
    kvns_s, kvns_r, kvew_s, kvew_r, wsc_s, wsc_r, g_s, g_r, wy_s, wy_r, wx_s, wx_r,
    rs_s, rs_r, dew_s, dew_r, dns_s, dns_r, load, store,
):
    t = lax.axis_index("tile")
    mp = lax.axis_index("mp")
    core = lax.rem(t, 2)
    x = lax.rem(t // 2, NX)
    z_hi = lax.rem(t // COLUMNS, 2)
    y = t // (2 * COLUMNS)
    row = t // COLUMNS
    col = lax.rem(t, COLUMNS)
    north = (lax.rem(t + 128 - COLUMNS, 128), mp)
    south = (lax.rem(t + COLUMNS, 128), mp)
    east = (row * COLUMNS + lax.rem(col + 1, COLUMNS), mp)
    west = (row * COLUMNS + lax.rem(col + 7, COLUMNS), mp)
    other = (t + 1 - 2 * core, mp)

    half, within = y // 4, lax.rem(y, 4)
    y_to = jnp.where(z_hi == 0, y, lax.rem(4 * half + 7 - within, NY))
    scatter_to = [(tile_of(x, y_to, hi, mp // 2), 2 * half + lax.rem(mp, 2)) for hi in range(2)]
    b_in, b_hi = held_block(y, mp)
    scatter_from = [
        (tile_of(x, 4 * (mp // 2) + b_in, b_hi, c), lax.rem(mp, 2) + 2 * core) for c in range(2)
    ]
    side = lax.rem(mp, 2)
    pair = mp + 1 - 2 * side
    far = lax.rem(mp + 2, 4)
    block_of_heads = side + 2 * core

    def y_peer(d):
        return (tile_of(x, lax.rem(y + d, NY), z_hi, core), mp)

    def x_peer(e):
        return (tile_of(lax.rem(x + e, NX), y, z_hi, core), mp)

    greeted = [north, south, east, west] + scatter_to + scatter_from
    greeted += [y_peer(d) for d in range(1, NY)] + [x_peer(e) for e in range(1, NX)]
    greeted += [(t, pair), (t, far), (other[0], far)]
    barrier = pltpu.get_barrier_semaphore()
    for device in greeted:
        pl.semaphore_signal(barrier, inc=1, device_id=device, device_id_type=MESH)

    loads = []
    for i, (src, dst) in enumerate(
        ((w_hbm, w), (k_hbm, k), (v_hbm, v), (g_hbm, gall.at[side, core]), (q_hbm, q))
    ):
        loads.append(pltpu.make_async_copy(src, dst, load.at[i]))
        loads[-1].start()

    loads[0].wait()
    wpad[0:24, :] = w[...]
    wpad[24:32, :] = jnp.zeros((8, HEADS_DEV * HD), jnp.bfloat16)
    loads[1].wait()
    loads[2].wait()
    for h in range(HEADS_DEV):
        lanes = slice(h * HD, (h + 1) * HD)
        for kv, ref in enumerate((k, v)):
            halves = to_halves(ref[:, lanes])
            for i in range(2):
                win[h, kv, 1 + i, STRIP : STRIP + 128, :] = halves[i]
    loads[3].wait()
    pl.semaphore_wait(barrier, len(greeted))

    def remote(src, dst, send, recv, device):
        return pltpu.make_async_remote_copy(src, dst, send, recv, device_id=device, device_id_type=MESH)

    sent = []

    def send(src, dst, send_sem, recv_sem, device):
        copy = remote(src, dst, send_sem, recv_sem, device)
        copy.start()
        sent.append(copy)

    def wait_recv(dst, recv_sem):
        remote(dst, dst, recv_sem, recv_sem, other).wait_recv()

    for hi in range(2):
        device = scatter_to[hi]
        mine = (device[0] == t) & (device[1] == mp)

        @pl.when(mine)
        def _():
            pltpu.make_async_copy(wpad, stage.at[core], wsc_r.at[core]).start()

        @pl.when(jnp.logical_not(mine))
        def _():
            remote(wpad, stage.at[core], wsc_s.at[hi], wsc_r.at[core], device).start()

    def top(h):
        return win.at[h, :, 1:3, STRIP : 2 * STRIP]

    def bottom(h):
        return win.at[h, :, 1:3, 2 * STRIP : 3 * STRIP]

    def halo_n(h):
        return win.at[h, :, 1:3, 0:STRIP]

    def halo_s(h):
        return win.at[h, :, 1:3, 3 * STRIP : 4 * STRIP]

    mine_g = gall.at[side, core]
    near_g = gall.at[1 - side, core]
    send(mine_g, mine_g, g_s.at[0], g_r.at[0], (t, pair))
    send(mine_g, mine_g, g_s.at[1], g_r.at[1], other)

    def halo_rows(h):
        send(top(h), halo_s(h), kvns_s.at[h, 0], kvns_r.at[h, 0], north)
        send(bottom(h), halo_n(h), kvns_s.at[h, 1], kvns_r.at[h, 1], south)

    def halo_columns(h):
        wait_recv(halo_s(h), kvns_r.at[h, 0])
        wait_recv(halo_n(h), kvns_r.at[h, 1])
        send(win.at[h, :, 1], win.at[h, :, 3], kvew_s.at[h, 0], kvew_r.at[h, 0], west)
        send(win.at[h, :, 2], win.at[h, :, 0], kvew_s.at[h, 1], kvew_r.at[h, 1], east)

    halo_rows(0)
    halo_rows(1)

    for c in range(2):
        wait_recv(stage.at[c], wsc_r.at[c])

    def block_at(x_at, y_at):
        inside, hi = held_block(y_at, mp)
        begin = pl.multiple_of(48 * ((inside * 2 + hi) * NX + x_at), 16)
        return wbuf.at[:, pl.ds(begin, 48), :]

    block = stage[:, 0:24, :].astype(jnp.float32).reshape(48, HEADS_DEV * HD).astype(jnp.bfloat16)
    begin = pl.multiple_of(48 * ((b_in * 2 + b_hi) * NX + x), 16)
    for h in range(HEADS_DEV):
        wbuf[h, pl.ds(begin, 48), :] = block[:, h * HD : (h + 1) * HD]
    my_block = block_at(x, y)
    y_order = (1, 7, 2, 6, 3, 5, 4)
    x_order = (1, 3, 2)
    for d in y_order:
        send(my_block, my_block, wy_s.at[d], wy_r.at[d], y_peer(d))
    for e in x_order:
        send(my_block, my_block, wx_s.at[0, e], wx_r.at[0, e], x_peer(e))
    for d in y_order:
        theirs = block_at(x, lax.rem(y + NY - d, NY))
        wait_recv(theirs, wy_r.at[d])
        for e in x_order:
            send(theirs, theirs, wx_s.at[d, e], wx_r.at[d, e], x_peer(e))
    halo_rows(2)

    wait_recv(near_g, g_r.at[0])
    send(near_g, near_g, g_s.at[2], g_r.at[2], other)
    wait_recv(gall.at[side, 1 - core], g_r.at[1])
    wait_recv(gall.at[1 - side, 1 - core], g_r.at[2])

    for d in (0,) + y_order:
        for e in x_order:
            theirs = block_at(lax.rem(x + NX - e, NX), lax.rem(y + NY - d, NY))
            wait_recv(theirs, wx_r.at[d, e])

    slot = jnp.where(block_of_heads == mp, 0, 1)

    def part_copy(h, c):
        device = (t - core + c, block_of_heads)
        mine = (block_of_heads == mp) & (core == c)
        return mine, remote(part.at[h, c], arrived.at[h, slot], rs_s.at[h, c], rs_r.at[h, slot], device)

    def share(h):
        total = jnp.zeros((2 * TOK, HD), jnp.float32)
        for i in range(2):
            total = total + jnp.dot(
                gall[i].reshape(2 * TOK, K_DEV),
                wbuf[h, i * K_DEV : (i + 1) * K_DEV, :],
                preferred_element_type=jnp.float32,
            )
        part[h] = total.reshape(2, TOK, HD).astype(jnp.bfloat16)
        for c in range(2):
            mine, copy = part_copy(h, c)

            @pl.when(mine)
            def _():
                pltpu.make_async_copy(part.at[h, c], arrived.at[h, slot], rs_r.at[h, slot]).start()

            @pl.when(jnp.logical_not(mine))
            def _():
                copy.start()

    share(0)
    share(1)
    share(2)

    halo_columns(0)
    loads[4].wait()
    key_at = lax.broadcasted_iota(jnp.int32, (KEYS, CHUNK), 0)
    group = key_at // 256
    key_row = lax.rem(key_at, 256) // 8
    valid = (
        ((group > 0) | (col > 0))
        & ((group < 3) | (col < COLUMNS - 1))
        & ((key_row >= 8) | (row > 0))
        & ((key_row < 24) | (row < ROWS - 1))
    )
    bias[...] = jnp.where(valid, 0.0, -1e30)

    def softmax(h):
        wait_recv(win.at[h, :, 3], kvew_r.at[h, 0])
        wait_recv(win.at[h, :, 0], kvew_r.at[h, 1])
        keys = win[h, 0].reshape(KEYS, HD)
        for i in range(2):
            rows = slice(i * CHUNK, (i + 1) * CHUNK)
            scores = lax.dot_general(
                keys, q[rows, h * HD : (h + 1) * HD], LAST, preferred_element_type=jnp.float32
            )
            scores = scores * (SCALE * LOG2E) + bias[...]
            unnormed = jnp.exp2(scores - jnp.max(scores, axis=0, keepdims=True))
            prob[h, i] = unnormed * (1.0 / jnp.sum(unnormed, axis=0, keepdims=True))

    stores = []

    def leave(i, ref, h):
        copy = pltpu.make_async_copy(out.at[i, h], ref.at[:, h * HD : (h + 1) * HD], store.at[i, h])
        copy.start()
        stores.append(copy)

    def spread_columns(h):
        send(ew_out.at[h, 0], ew_in.at[h, 0], dew_s.at[h, 0], dew_r.at[h, 0], west)
        send(ew_out.at[h, 1], ew_in.at[h, 1], dew_s.at[h, 1], dew_r.at[h, 1], east)

    def spread_rows(h):
        wait_recv(ew_in.at[h, 0], dew_r.at[h, 0])
        wait_recv(ew_in.at[h, 1], dew_r.at[h, 1])
        for kv in range(2):
            dwin[h, kv, 2] = dwin[h, kv, 2] + ew_in[h, 0, kv].astype(jnp.float32)
            dwin[h, kv, 1] = dwin[h, kv, 1] + ew_in[h, 1, kv].astype(jnp.float32)
            for i in range(2):
                ns_out[h, 0, kv, i] = dwin[h, kv, 1 + i, 0:STRIP].astype(jnp.bfloat16)
                ns_out[h, 1, kv, i] = dwin[h, kv, 1 + i, 3 * STRIP : 4 * STRIP].astype(jnp.bfloat16)
        send(ns_out.at[h, 0], ns_in.at[h, 0], dns_s.at[h, 0], dns_r.at[h, 0], north)
        send(ns_out.at[h, 1], ns_in.at[h, 1], dns_s.at[h, 1], dns_r.at[h, 1], south)

    def backward(h):
        lanes = slice(h * HD, (h + 1) * HD)
        total = jnp.zeros((TOK, HD), jnp.float32)
        for s in range(2):
            wait_recv(arrived.at[h, s], rs_r.at[h, s])
            total = total + arrived[h, s].astype(jnp.float32)
        cotangent = total.astype(jnp.bfloat16)
        keys = win[h, 0].reshape(KEYS, HD)
        values = win[h, 1].reshape(KEYS, HD)
        for i in range(2):
            rows = slice(i * CHUNK, (i + 1) * CHUNK)
            attention = prob[h, i]
            grad_attention = lax.dot_general(
                values, cotangent[rows], LAST, preferred_element_type=jnp.float32
            )
            row_total = jnp.sum(attention * grad_attention, axis=0, keepdims=True)
            grad_s[:, rows] = (attention * (grad_attention - row_total) * SCALE).astype(jnp.bfloat16)
            prob_low[:, rows] = attention.astype(jnp.bfloat16)
        dwin[h, 0] = jnp.dot(
            grad_s[...], q[:, lanes], preferred_element_type=jnp.float32
        ).reshape(4, 256, HD)
        dwin[h, 1] = jnp.dot(
            prob_low[...], cotangent, preferred_element_type=jnp.float32
        ).reshape(4, 256, HD)
        for kv in range(2):
            ew_out[h, 0, kv] = dwin[h, kv, 0].astype(jnp.bfloat16)
            ew_out[h, 1, kv] = dwin[h, kv, 3].astype(jnp.bfloat16)
        spread_columns(h)
        out[0, h] = lax.dot_general(
            grad_s[...], keys, FIRST, preferred_element_type=jnp.float32
        ).astype(jnp.bfloat16)
        leave(0, dq_hbm, h)

    def finish(h):
        wait_recv(ns_in.at[h, 0], dns_r.at[h, 0])
        wait_recv(ns_in.at[h, 1], dns_r.at[h, 1])
        for kv, ref in enumerate((dk_hbm, dv_hbm)):
            halves = []
            for i in range(2):
                upper = dwin[h, kv, 1 + i, STRIP : 2 * STRIP] + ns_in[h, 1, kv, i].astype(jnp.float32)
                lower = dwin[h, kv, 1 + i, 2 * STRIP : 3 * STRIP] + ns_in[h, 0, kv, i].astype(jnp.float32)
                halves.append(jnp.concatenate([upper, lower], axis=0).reshape(16, 8, HD))
            out[1 + kv, h] = jnp.stack(halves, axis=1).reshape(TOK, HD).astype(jnp.bfloat16)
            leave(1 + kv, ref, h)

    softmax(0)
    halo_columns(1)
    backward(0)
    softmax(1)
    halo_columns(2)
    spread_rows(0)
    backward(1)
    softmax(2)
    spread_rows(1)
    backward(2)
    spread_rows(2)
    for h in range(HEADS_DEV):
        finish(h)

    for copy in sent:
        copy.wait_send()
    for copy in stores:
        copy.wait()
    for hi in range(2):
        device = scatter_to[hi]
        mine = (device[0] == t) & (device[1] == mp)

        @pl.when(jnp.logical_not(mine))
        def _():
            remote(wpad, stage.at[core], wsc_s.at[hi], wsc_r.at[core], device).wait_send()

    for h in range(HEADS_DEV):
        for c in range(2):
            mine, copy = part_copy(h, c)

            @pl.when(jnp.logical_not(mine))
            def _():
                copy.wait_send()


def hand_over(a, b, c, a_out, b_out, c_out, held, sem):
    into = [pltpu.make_async_copy(src, held.at[i], sem.at[0, i]) for i, src in enumerate((a, b, c))]
    out_of = [pltpu.make_async_copy(held.at[i], dst, sem.at[1, i]) for i, dst in enumerate((a_out, b_out, c_out))]
    for copy in into:
        copy.start()
    for first, second in zip(into, out_of):
        first.wait()
        second.start()
    for copy in out_of:
        copy.wait()


def shards(query, key, value, grad_y, w_out):
    bf16, f32 = jnp.bfloat16, jnp.float32
    dma = pltpu.SemaphoreType.DMA
    out = jax.ShapeDtypeStruct(query.shape, bf16)
    hbm = pl.BlockSpec(memory_space=pltpu.HBM)
    grads = pl.pallas_call(
        kernel,
        name="tiled_attention_backward",
        out_shape=(out, out, out),
        in_specs=[hbm] * 5,
        out_specs=(hbm,) * 3,
        scratch_shapes=[
            pltpu.VMEM((HEADS_DEV, 2, 4, 256, HD), bf16),
            pltpu.VMEM((32, HEADS_DEV * HD), bf16),
            pltpu.VMEM((2, 32, HEADS_DEV * HD), bf16),
            pltpu.VMEM((HEADS_DEV, K_PAIR, HD), bf16),
            pltpu.VMEM((2, 2, TOK, K_DEV), bf16),
            pltpu.VMEM((HEADS_DEV, 2, TOK, HD), bf16),
            pltpu.VMEM((HEADS_DEV, 2, TOK, HD), bf16),
            pltpu.VMEM((KEYS, CHUNK), f32),
            pltpu.VMEM((HEADS_DEV, 2, KEYS, CHUNK), f32),
            pltpu.VMEM((KEYS, TOK), bf16),
            pltpu.VMEM((KEYS, TOK), bf16),
            pltpu.VMEM((HEADS_DEV, 2, 4, 256, HD), f32),
            pltpu.VMEM((HEADS_DEV, 2, 2, 256, HD), bf16),
            pltpu.VMEM((HEADS_DEV, 2, 2, 256, HD), bf16),
            pltpu.VMEM((HEADS_DEV, 2, 2, 2, STRIP, HD), bf16),
            pltpu.VMEM((HEADS_DEV, 2, 2, 2, STRIP, HD), bf16),
            pltpu.VMEM(query.shape, bf16),
            pltpu.VMEM(key.shape, bf16),
            pltpu.VMEM(value.shape, bf16),
            pltpu.VMEM(w_out.shape, bf16),
            pltpu.VMEM((3, HEADS_DEV, TOK, HD), bf16),
            dma((HEADS_DEV, 2)), dma((HEADS_DEV, 2)),
            dma((HEADS_DEV, 2)), dma((HEADS_DEV, 2)),
            dma((2,)), dma((2,)),
            dma((3,)), dma((3,)),
            dma((NY,)), dma((NY,)),
            dma((NY, NX)), dma((NY, NX)),
            dma((HEADS_DEV, 2)), dma((HEADS_DEV, 2)),
            dma((HEADS_DEV, 2)), dma((HEADS_DEV, 2)),
            dma((HEADS_DEV, 2)), dma((HEADS_DEV, 2)),
            dma((5,)),
            dma((3, HEADS_DEV)),
        ],
        compiler_params=pltpu.CompilerParams(
            collective_id=0, has_side_effects=True, vmem_limit_bytes=60 * 1024 * 1024
        ),
    )(query, key, value, grad_y, w_out)
    return pl.pallas_call(
        hand_over,
        name="hand_over",
        out_shape=(out, out, out),
        in_specs=[hbm] * 3,
        out_specs=(hbm,) * 3,
        scratch_shapes=[pltpu.VMEM((3,) + query.shape, bf16), dma((2, 3))],
        compiler_params=pltpu.CompilerParams(vmem_limit_bytes=60 * 1024 * 1024),
    )(*grads)


def solution(mesh):
    spec = P("tile", "mp")
    return jax.shard_map(
        shards, mesh=mesh, in_specs=(spec,) * 5, out_specs=(spec,) * 3, check_vma=False
    )
```

```python
import jax
import jax.numpy as jnp
from jax import lax
from jax.experimental import pallas as pl
from jax.experimental.pallas import tpu as pltpu
from jax.sharding import PartitionSpec as P

HD = 128
HEADS_DEV = 3
COLUMNS = 8
ROWS = 16
NY = 8
NX = 4
TOK = 256
STRIP = 64
KEYS = 1024
CHUNK = 128
K_DEV = 768
K_PAIR = 1536
LOG2E = 1.4426950408889634
SCALE = HD ** (-0.5)
MESH = pl.DeviceIdType.MESH
LAST = (((1,), (1,)), ((), ()))
FIRST = (((0,), (0,)), ((), ()))


def tile_of(x, y, z_hi, core):
    return ((y * 2 + z_hi) * NX + x) * 2 + core


def held_block(y, mp):
    p = lax.rem(y - 4 * (mp // 2) + NY, NY)
    return jnp.where(p < 4, p, 7 - p), jnp.where(p < 4, 0, 1)


def to_halves(tokens):
    wide = tokens.astype(jnp.float32).reshape(16, 2, 8, HD)
    return [wide[:, i].reshape(128, HD).astype(jnp.bfloat16) for i in range(2)]


def kernel(
    q_hbm, k_hbm, v_hbm, g_hbm, w_hbm, dq_ref, dk_ref, dv_ref,
    win, wpad, stage, wbuf, gall, part, arrived, bias, prob, grad_s, prob_low, dwin,
    ew_out, ew_in, ns_out, ns_in, q, k, v, w,
    kvns_s, kvns_r, kvew_s, kvew_r, wsc_s, wsc_r, g_s, g_r, wy_s, wy_r, wx_s, wx_r,
    rs_s, rs_r, dew_s, dew_r, dns_s, dns_r, load,
):
    t = lax.axis_index("tile")
    mp = lax.axis_index("mp")
    core = lax.rem(t, 2)
    x = lax.rem(t // 2, NX)
    z_hi = lax.rem(t // COLUMNS, 2)
    y = t // (2 * COLUMNS)
    row = t // COLUMNS
    col = lax.rem(t, COLUMNS)
    north = (lax.rem(t + 128 - COLUMNS, 128), mp)
    south = (lax.rem(t + COLUMNS, 128), mp)
    east = (row * COLUMNS + lax.rem(col + 1, COLUMNS), mp)
    west = (row * COLUMNS + lax.rem(col + 7, COLUMNS), mp)
    other = (t + 1 - 2 * core, mp)

    half, within = y // 4, lax.rem(y, 4)
    y_to = jnp.where(z_hi == 0, y, lax.rem(4 * half + 7 - within, NY))
    scatter_to = [(tile_of(x, y_to, hi, mp // 2), 2 * half + lax.rem(mp, 2)) for hi in range(2)]
    b_in, b_hi = held_block(y, mp)
    scatter_from = [
        (tile_of(x, 4 * (mp // 2) + b_in, b_hi, c), lax.rem(mp, 2) + 2 * core) for c in range(2)
    ]
    side = lax.rem(mp, 2)
    pair = mp + 1 - 2 * side
    far = lax.rem(mp + 2, 4)
    block_of_heads = side + 2 * core

    def y_peer(d):
        return (tile_of(x, lax.rem(y + d, NY), z_hi, core), mp)

    def x_peer(e):
        return (tile_of(lax.rem(x + e, NX), y, z_hi, core), mp)

    greeted = [north, south, east, west] + scatter_to + scatter_from
    greeted += [y_peer(d) for d in range(1, NY)] + [x_peer(e) for e in range(1, NX)]
    greeted += [(t, pair), (t, far), (other[0], far)]
    barrier = pltpu.get_barrier_semaphore()
    for device in greeted:
        pl.semaphore_signal(barrier, inc=1, device_id=device, device_id_type=MESH)

    loads = []
    for i, (src, dst) in enumerate(
        ((w_hbm, w), (k_hbm, k), (v_hbm, v), (g_hbm, gall.at[side, core]), (q_hbm, q))
    ):
        loads.append(pltpu.make_async_copy(src, dst, load.at[i]))
        loads[-1].start()

    loads[0].wait()
    wpad[0:24, :] = w[...]
    wpad[24:32, :] = jnp.zeros((8, HEADS_DEV * HD), jnp.bfloat16)
    loads[1].wait()
    loads[2].wait()
    for h in range(HEADS_DEV):
        lanes = slice(h * HD, (h + 1) * HD)
        for kv, ref in enumerate((k, v)):
            halves = to_halves(ref[:, lanes])
            for i in range(2):
                win[h, kv, 1 + i, STRIP : STRIP + 128, :] = halves[i]
    loads[3].wait()
    pl.semaphore_wait(barrier, len(greeted))

    def remote(src, dst, send, recv, device):
        return pltpu.make_async_remote_copy(src, dst, send, recv, device_id=device, device_id_type=MESH)

    sent = []

    def send(src, dst, send_sem, recv_sem, device):
        copy = remote(src, dst, send_sem, recv_sem, device)
        copy.start()
        sent.append(copy)

    def wait_recv(dst, recv_sem):
        remote(dst, dst, recv_sem, recv_sem, other).wait_recv()

    for hi in range(2):
        device = scatter_to[hi]
        mine = (device[0] == t) & (device[1] == mp)

        @pl.when(mine)
        def _():
            pltpu.make_async_copy(wpad, stage.at[core], wsc_r.at[core]).start()

        @pl.when(jnp.logical_not(mine))
        def _():
            remote(wpad, stage.at[core], wsc_s.at[hi], wsc_r.at[core], device).start()

    def top(h):
        return win.at[h, :, 1:3, STRIP : 2 * STRIP]

    def bottom(h):
        return win.at[h, :, 1:3, 2 * STRIP : 3 * STRIP]

    def halo_n(h):
        return win.at[h, :, 1:3, 0:STRIP]

    def halo_s(h):
        return win.at[h, :, 1:3, 3 * STRIP : 4 * STRIP]

    mine_g = gall.at[side, core]
    near_g = gall.at[1 - side, core]
    send(mine_g, mine_g, g_s.at[0], g_r.at[0], (t, pair))
    send(mine_g, mine_g, g_s.at[1], g_r.at[1], other)

    def halo_rows(h):
        send(top(h), halo_s(h), kvns_s.at[h, 0], kvns_r.at[h, 0], north)
        send(bottom(h), halo_n(h), kvns_s.at[h, 1], kvns_r.at[h, 1], south)

    def halo_columns(h):
        wait_recv(halo_s(h), kvns_r.at[h, 0])
        wait_recv(halo_n(h), kvns_r.at[h, 1])
        send(win.at[h, :, 1], win.at[h, :, 3], kvew_s.at[h, 0], kvew_r.at[h, 0], west)
        send(win.at[h, :, 2], win.at[h, :, 0], kvew_s.at[h, 1], kvew_r.at[h, 1], east)

    halo_rows(0)
    halo_rows(1)

    key_at = lax.broadcasted_iota(jnp.int32, (KEYS, CHUNK), 0)
    group = key_at // 256
    key_row = lax.rem(key_at, 256) // 8
    valid = (
        ((group > 0) | (col > 0))
        & ((group < 3) | (col < COLUMNS - 1))
        & ((key_row >= 8) | (row > 0))
        & ((key_row < 24) | (row < ROWS - 1))
    )
    bias[...] = jnp.where(valid, 0.0, -1e30)

    for c in range(2):
        wait_recv(stage.at[c], wsc_r.at[c])

    def block_at(x_at, y_at):
        inside, hi = held_block(y_at, mp)
        begin = pl.multiple_of(48 * ((inside * 2 + hi) * NX + x_at), 16)
        return wbuf.at[:, pl.ds(begin, 48), :]

    block = stage[:, 0:24, :].astype(jnp.float32).reshape(48, HEADS_DEV * HD).astype(jnp.bfloat16)
    begin = pl.multiple_of(48 * ((b_in * 2 + b_hi) * NX + x), 16)
    for h in range(HEADS_DEV):
        wbuf[h, pl.ds(begin, 48), :] = block[:, h * HD : (h + 1) * HD]
    my_block = block_at(x, y)
    y_order = (1, 7, 2, 6, 3, 5, 4)
    x_order = (1, 3, 2)
    for d in y_order:
        send(my_block, my_block, wy_s.at[d], wy_r.at[d], y_peer(d))
    for e in x_order:
        send(my_block, my_block, wx_s.at[0, e], wx_r.at[0, e], x_peer(e))
    for d in y_order:
        theirs = block_at(x, lax.rem(y + NY - d, NY))
        wait_recv(theirs, wy_r.at[d])
        for e in x_order:
            send(theirs, theirs, wx_s.at[d, e], wx_r.at[d, e], x_peer(e))
    halo_rows(2)

    wait_recv(near_g, g_r.at[0])
    send(near_g, near_g, g_s.at[2], g_r.at[2], other)
    wait_recv(gall.at[side, 1 - core], g_r.at[1])
    wait_recv(gall.at[1 - side, 1 - core], g_r.at[2])

    for d in (0,) + y_order:
        for e in x_order:
            theirs = block_at(lax.rem(x + NX - e, NX), lax.rem(y + NY - d, NY))
            wait_recv(theirs, wx_r.at[d, e])

    slot = jnp.where(block_of_heads == mp, 0, 1)

    def part_copy(h, c):
        device = (t - core + c, block_of_heads)
        mine = (block_of_heads == mp) & (core == c)
        return mine, remote(part.at[h, c], arrived.at[h, slot], rs_s.at[h, c], rs_r.at[h, slot], device)

    def share(h):
        total = jnp.zeros((2 * TOK, HD), jnp.float32)
        for i in range(2):
            total = total + jnp.dot(
                gall[i].reshape(2 * TOK, K_DEV),
                wbuf[h, i * K_DEV : (i + 1) * K_DEV, :],
                preferred_element_type=jnp.float32,
            )
        part[h] = total.reshape(2, TOK, HD).astype(jnp.bfloat16)
        for c in range(2):
            mine, copy = part_copy(h, c)

            @pl.when(mine)
            def _():
                pltpu.make_async_copy(part.at[h, c], arrived.at[h, slot], rs_r.at[h, slot]).start()

            @pl.when(jnp.logical_not(mine))
            def _():
                copy.start()

    share(0)
    share(1)
    share(2)

    halo_columns(0)
    loads[4].wait()

    def softmax(h):
        wait_recv(win.at[h, :, 3], kvew_r.at[h, 0])
        wait_recv(win.at[h, :, 0], kvew_r.at[h, 1])
        keys = win[h, 0].reshape(KEYS, HD)
        for i in range(2):
            rows = slice(i * CHUNK, (i + 1) * CHUNK)
            scores = lax.dot_general(
                keys, q[rows, h * HD : (h + 1) * HD], LAST, preferred_element_type=jnp.float32
            )
            scores = scores * (SCALE * LOG2E) + bias[...]
            unnormed = jnp.exp2(scores - jnp.max(scores, axis=0, keepdims=True))
            prob[h, i] = unnormed * (1.0 / jnp.sum(unnormed, axis=0, keepdims=True))

    def spread_columns(h):
        send(ew_out.at[h, 0], ew_in.at[h, 0], dew_s.at[h, 0], dew_r.at[h, 0], west)
        send(ew_out.at[h, 1], ew_in.at[h, 1], dew_s.at[h, 1], dew_r.at[h, 1], east)

    def spread_rows(h):
        wait_recv(ew_in.at[h, 0], dew_r.at[h, 0])
        wait_recv(ew_in.at[h, 1], dew_r.at[h, 1])
        for kv in range(2):
            dwin[h, kv, 2] = dwin[h, kv, 2] + ew_in[h, 0, kv].astype(jnp.float32)
            dwin[h, kv, 1] = dwin[h, kv, 1] + ew_in[h, 1, kv].astype(jnp.float32)
            for i in range(2):
                ns_out[h, 0, kv, i] = dwin[h, kv, 1 + i, 0:STRIP].astype(jnp.bfloat16)
                ns_out[h, 1, kv, i] = dwin[h, kv, 1 + i, 3 * STRIP : 4 * STRIP].astype(jnp.bfloat16)
        send(ns_out.at[h, 0], ns_in.at[h, 0], dns_s.at[h, 0], dns_r.at[h, 0], north)
        send(ns_out.at[h, 1], ns_in.at[h, 1], dns_s.at[h, 1], dns_r.at[h, 1], south)

    def backward(h):
        lanes = slice(h * HD, (h + 1) * HD)
        total = jnp.zeros((TOK, HD), jnp.float32)
        for s in range(2):
            wait_recv(arrived.at[h, s], rs_r.at[h, s])
            total = total + arrived[h, s].astype(jnp.float32)
        cotangent = total.astype(jnp.bfloat16)
        keys = win[h, 0].reshape(KEYS, HD)
        values = win[h, 1].reshape(KEYS, HD)
        for i in range(2):
            rows = slice(i * CHUNK, (i + 1) * CHUNK)
            attention = prob[h, i]
            grad_attention = lax.dot_general(
                values, cotangent[rows], LAST, preferred_element_type=jnp.float32
            )
            row_total = jnp.sum(attention * grad_attention, axis=0, keepdims=True)
            grad_s[:, rows] = (attention * (grad_attention - row_total) * SCALE).astype(jnp.bfloat16)
            prob_low[:, rows] = attention.astype(jnp.bfloat16)
        dwin[h, 0] = jnp.dot(
            grad_s[...], q[:, lanes], preferred_element_type=jnp.float32
        ).reshape(4, 256, HD)
        dwin[h, 1] = jnp.dot(
            prob_low[...], cotangent, preferred_element_type=jnp.float32
        ).reshape(4, 256, HD)
        for kv in range(2):
            ew_out[h, 0, kv] = dwin[h, kv, 0].astype(jnp.bfloat16)
            ew_out[h, 1, kv] = dwin[h, kv, 3].astype(jnp.bfloat16)
        spread_columns(h)
        dq_ref[:, lanes] = lax.dot_general(
            grad_s[...], keys, FIRST, preferred_element_type=jnp.float32
        ).astype(jnp.bfloat16)

    def finish(h):
        wait_recv(ns_in.at[h, 0], dns_r.at[h, 0])
        wait_recv(ns_in.at[h, 1], dns_r.at[h, 1])
        for kv, ref in enumerate((dk_ref, dv_ref)):
            halves = []
            for i in range(2):
                upper = dwin[h, kv, 1 + i, STRIP : 2 * STRIP] + ns_in[h, 1, kv, i].astype(jnp.float32)
                lower = dwin[h, kv, 1 + i, 2 * STRIP : 3 * STRIP] + ns_in[h, 0, kv, i].astype(jnp.float32)
                halves.append(jnp.concatenate([upper, lower], axis=0).reshape(16, 8, HD))
            ref[:, h * HD : (h + 1) * HD] = jnp.stack(halves, axis=1).reshape(TOK, HD).astype(jnp.bfloat16)

    softmax(0)
    halo_columns(1)
    backward(0)
    softmax(1)
    halo_columns(2)
    spread_rows(0)
    backward(1)
    softmax(2)
    spread_rows(1)
    backward(2)
    spread_rows(2)
    for h in range(HEADS_DEV - 1):
        finish(h)

    for copy in sent[:-2]:
        copy.wait_send()
    for hi in range(2):
        device = scatter_to[hi]
        mine = (device[0] == t) & (device[1] == mp)

        @pl.when(jnp.logical_not(mine))
        def _():
            remote(wpad, stage.at[core], wsc_s.at[hi], wsc_r.at[core], device).wait_send()

    for h in range(HEADS_DEV):
        for c in range(2):
            mine, copy = part_copy(h, c)

            @pl.when(jnp.logical_not(mine))
            def _():
                copy.wait_send()

    finish(HEADS_DEV - 1)
    for copy in sent[-2:]:
        copy.wait_send()


def hand_over(a, b, c, a_out, b_out, c_out, sem):
    copies = [
        pltpu.make_async_copy(src, dst, sem.at[i])
        for i, (src, dst) in enumerate(((a, a_out), (b, b_out), (c, c_out)))
    ]
    for copy in copies:
        copy.start()
    for copy in copies:
        copy.wait()


def shards(query, key, value, grad_y, w_out):
    bf16, f32 = jnp.bfloat16, jnp.float32
    dma = pltpu.SemaphoreType.DMA
    out = jax.ShapeDtypeStruct(query.shape, bf16)
    held = pltpu.VMEM(query.shape, bf16)
    vmem = pl.BlockSpec(memory_space=pltpu.VMEM)
    hbm = pl.BlockSpec(memory_space=pltpu.HBM)
    grads = pl.pallas_call(
        kernel,
        name="tiled_attention_backward",
        out_shape=(held, held, held),
        in_specs=[hbm] * 5,
        out_specs=(vmem,) * 3,
        scratch_shapes=[
            pltpu.VMEM((HEADS_DEV, 2, 4, 256, HD), bf16),
            pltpu.VMEM((32, HEADS_DEV * HD), bf16),
            pltpu.VMEM((2, 32, HEADS_DEV * HD), bf16),
            pltpu.VMEM((HEADS_DEV, K_PAIR, HD), bf16),
            pltpu.VMEM((2, 2, TOK, K_DEV), bf16),
            pltpu.VMEM((HEADS_DEV, 2, TOK, HD), bf16),
            pltpu.VMEM((HEADS_DEV, 2, TOK, HD), bf16),
            pltpu.VMEM((KEYS, CHUNK), f32),
            pltpu.VMEM((HEADS_DEV, 2, KEYS, CHUNK), f32),
            pltpu.VMEM((KEYS, TOK), bf16),
            pltpu.VMEM((KEYS, TOK), bf16),
            pltpu.VMEM((HEADS_DEV, 2, 4, 256, HD), f32),
            pltpu.VMEM((HEADS_DEV, 2, 2, 256, HD), bf16),
            pltpu.VMEM((HEADS_DEV, 2, 2, 256, HD), bf16),
            pltpu.VMEM((HEADS_DEV, 2, 2, 2, STRIP, HD), bf16),
            pltpu.VMEM((HEADS_DEV, 2, 2, 2, STRIP, HD), bf16),
            pltpu.VMEM(query.shape, bf16),
            pltpu.VMEM(key.shape, bf16),
            pltpu.VMEM(value.shape, bf16),
            pltpu.VMEM(w_out.shape, bf16),
            dma((HEADS_DEV, 2)), dma((HEADS_DEV, 2)),
            dma((HEADS_DEV, 2)), dma((HEADS_DEV, 2)),
            dma((2,)), dma((2,)),
            dma((3,)), dma((3,)),
            dma((NY,)), dma((NY,)),
            dma((NY, NX)), dma((NY, NX)),
            dma((HEADS_DEV, 2)), dma((HEADS_DEV, 2)),
            dma((HEADS_DEV, 2)), dma((HEADS_DEV, 2)),
            dma((HEADS_DEV, 2)), dma((HEADS_DEV, 2)),
            dma((5,)),
        ],
        compiler_params=pltpu.CompilerParams(
            collective_id=0, has_side_effects=True, vmem_limit_bytes=60 * 1024 * 1024
        ),
    )(query, key, value, grad_y, w_out)
    return pl.pallas_call(
        hand_over,
        name="hand_over",
        out_shape=(out, out, out),
        in_specs=[vmem] * 3,
        out_specs=(hbm,) * 3,
        scratch_shapes=[dma((3,))],
    )(*(pltpu.with_memory_space_constraint(g, pltpu.VMEM) for g in grads))


def solution(mesh):
    spec = P("tile", "mp")
    return jax.shard_map(
        shards, mesh=mesh, in_specs=(spec,) * 5, out_specs=(spec,) * 3, check_vma=False
    )
```

```python
import jax
import jax.numpy as jnp
from jax import lax
from jax.experimental import pallas as pl
from jax.experimental.pallas import tpu as pltpu
from jax.sharding import PartitionSpec as P

HD = 128
HEADS_DEV = 3
COLUMNS = 8
ROWS = 16
NY = 8
NX = 4
TOK = 256
STRIP = 64
KEYS = 1024
CHUNK = 128
K_DEV = 768
K_PAIR = 1536
LOG2E = 1.4426950408889634
SCALE = HD ** (-0.5)
MESH = pl.DeviceIdType.MESH
LAST = (((1,), (1,)), ((), ()))
FIRST = (((0,), (0,)), ((), ()))


def tile_of(x, y, z_hi, core):
    return ((y * 2 + z_hi) * NX + x) * 2 + core


def held_block(y, mp):
    p = lax.rem(y - 4 * (mp // 2) + NY, NY)
    return jnp.where(p < 4, p, 7 - p), jnp.where(p < 4, 0, 1)


def to_halves(tokens):
    wide = tokens.astype(jnp.float32).reshape(16, 2, 8, HD)
    return [wide[:, i].reshape(128, HD).astype(jnp.bfloat16) for i in range(2)]


def kernel(
    q_hbm, k_hbm, v_hbm, g_hbm, w_hbm, dq_ref, dk_ref, dv_ref,
    win, wpad, stage, wbuf, gall, part, arrived, bias, prob, grad_s, prob_low, dwin,
    ew_out, ew_in, ns_out, ns_in, q, k, v,
    kvns_s, kvns_r, kvew_s, kvew_r, wsc_s, wsc_r, g_s, g_r, wy_s, wy_r, wx_s, wx_r,
    rs_s, rs_r, dew_s, dew_r, dns_s, dns_r, load,
):
    t = lax.axis_index("tile")
    mp = lax.axis_index("mp")
    core = lax.rem(t, 2)
    x = lax.rem(t // 2, NX)
    z_hi = lax.rem(t // COLUMNS, 2)
    y = t // (2 * COLUMNS)
    row = t // COLUMNS
    col = lax.rem(t, COLUMNS)
    north = (lax.rem(t + 128 - COLUMNS, 128), mp)
    south = (lax.rem(t + COLUMNS, 128), mp)
    east = (row * COLUMNS + lax.rem(col + 1, COLUMNS), mp)
    west = (row * COLUMNS + lax.rem(col + 7, COLUMNS), mp)
    other = (t + 1 - 2 * core, mp)

    half, within = y // 4, lax.rem(y, 4)
    y_to = jnp.where(z_hi == 0, y, lax.rem(4 * half + 7 - within, NY))
    scatter_to = [(tile_of(x, y_to, hi, mp // 2), 2 * half + lax.rem(mp, 2)) for hi in range(2)]
    b_in, b_hi = held_block(y, mp)
    scatter_from = [
        (tile_of(x, 4 * (mp // 2) + b_in, b_hi, c), lax.rem(mp, 2) + 2 * core) for c in range(2)
    ]
    side = lax.rem(mp, 2)
    pair = mp + 1 - 2 * side
    far = lax.rem(mp + 2, 4)
    block_of_heads = side + 2 * core

    def y_peer(d):
        return (tile_of(x, lax.rem(y + d, NY), z_hi, core), mp)

    def x_peer(e):
        return (tile_of(lax.rem(x + e, NX), y, z_hi, core), mp)

    greeted = [north, south, east, west] + scatter_to + scatter_from
    greeted += [y_peer(d) for d in range(1, NY)] + [x_peer(e) for e in range(1, NX)]
    greeted += [(t, pair), (t, far), (other[0], far)]
    barrier = pltpu.get_barrier_semaphore()
    for device in greeted:
        pl.semaphore_signal(barrier, inc=1, device_id=device, device_id_type=MESH)

    loads = []
    for i, (src, dst) in enumerate(
        ((w_hbm, wpad), (k_hbm, k), (v_hbm, v), (g_hbm, gall.at[side, core]), (q_hbm, q))
    ):
        loads.append(pltpu.make_async_copy(src, dst, load.at[i]))
        loads[-1].start()

    loads[0].wait()
    loads[1].wait()
    loads[2].wait()
    for h in range(HEADS_DEV):
        lanes = slice(h * HD, (h + 1) * HD)
        for kv, ref in enumerate((k, v)):
            halves = to_halves(ref[:, lanes])
            for i in range(2):
                win[h, kv, 1 + i, STRIP : STRIP + 128, :] = halves[i]
    loads[3].wait()
    pl.semaphore_wait(barrier, len(greeted))

    def remote(src, dst, send, recv, device):
        return pltpu.make_async_remote_copy(src, dst, send, recv, device_id=device, device_id_type=MESH)

    sent = []

    def send(src, dst, send_sem, recv_sem, device):
        copy = remote(src, dst, send_sem, recv_sem, device)
        copy.start()
        sent.append(copy)

    def wait_recv(dst, recv_sem):
        remote(dst, dst, recv_sem, recv_sem, other).wait_recv()

    for hi in range(2):
        device = scatter_to[hi]
        mine = (device[0] == t) & (device[1] == mp)

        @pl.when(mine)
        def _():
            pltpu.make_async_copy(wpad, stage.at[core], wsc_r.at[core]).start()

        @pl.when(jnp.logical_not(mine))
        def _():
            remote(wpad, stage.at[core], wsc_s.at[hi], wsc_r.at[core], device).start()

    def top(h):
        return win.at[h, :, 1:3, STRIP : 2 * STRIP]

    def bottom(h):
        return win.at[h, :, 1:3, 2 * STRIP : 3 * STRIP]

    def halo_n(h):
        return win.at[h, :, 1:3, 0:STRIP]

    def halo_s(h):
        return win.at[h, :, 1:3, 3 * STRIP : 4 * STRIP]

    mine_g = gall.at[side, core]
    near_g = gall.at[1 - side, core]
    send(mine_g, mine_g, g_s.at[0], g_r.at[0], (t, pair))
    send(mine_g, mine_g, g_s.at[1], g_r.at[1], other)

    def halo_rows(h):
        send(top(h), halo_s(h), kvns_s.at[h, 0], kvns_r.at[h, 0], north)
        send(bottom(h), halo_n(h), kvns_s.at[h, 1], kvns_r.at[h, 1], south)

    def halo_columns(h):
        wait_recv(halo_s(h), kvns_r.at[h, 0])
        wait_recv(halo_n(h), kvns_r.at[h, 1])
        send(win.at[h, :, 1], win.at[h, :, 3], kvew_s.at[h, 0], kvew_r.at[h, 0], west)
        send(win.at[h, :, 2], win.at[h, :, 0], kvew_s.at[h, 1], kvew_r.at[h, 1], east)

    halo_rows(0)
    halo_rows(1)

    key_at = lax.broadcasted_iota(jnp.int32, (KEYS, CHUNK), 0)
    group = key_at // 256
    key_row = lax.rem(key_at, 256) // 8
    valid = (
        ((group > 0) | (col > 0))
        & ((group < 3) | (col < COLUMNS - 1))
        & ((key_row >= 8) | (row > 0))
        & ((key_row < 24) | (row < ROWS - 1))
    )
    bias[...] = jnp.where(valid, 0.0, -1e30)

    for c in range(2):
        wait_recv(stage.at[c], wsc_r.at[c])

    def block_at(x_at, y_at):
        inside, hi = held_block(y_at, mp)
        begin = pl.multiple_of(48 * ((inside * 2 + hi) * NX + x_at), 16)
        return wbuf.at[:, pl.ds(begin, 48), :]

    block = stage[:, 0:24, :].astype(jnp.float32).reshape(48, HEADS_DEV * HD).astype(jnp.bfloat16)
    begin = pl.multiple_of(48 * ((b_in * 2 + b_hi) * NX + x), 16)
    for h in range(HEADS_DEV):
        wbuf[h, pl.ds(begin, 48), :] = block[:, h * HD : (h + 1) * HD]
    my_block = block_at(x, y)
    y_order = (1, 7, 2, 6, 3, 5, 4)
    x_order = (1, 3, 2)
    for d in y_order:
        send(my_block, my_block, wy_s.at[d], wy_r.at[d], y_peer(d))
    for e in x_order:
        send(my_block, my_block, wx_s.at[0, e], wx_r.at[0, e], x_peer(e))
    for d in y_order:
        theirs = block_at(x, lax.rem(y + NY - d, NY))
        wait_recv(theirs, wy_r.at[d])
        for e in x_order:
            send(theirs, theirs, wx_s.at[d, e], wx_r.at[d, e], x_peer(e))
    halo_rows(2)

    wait_recv(near_g, g_r.at[0])
    send(near_g, near_g, g_s.at[2], g_r.at[2], other)
    wait_recv(gall.at[side, 1 - core], g_r.at[1])
    wait_recv(gall.at[1 - side, 1 - core], g_r.at[2])

    for d in (0,) + y_order:
        for e in x_order:
            theirs = block_at(lax.rem(x + NX - e, NX), lax.rem(y + NY - d, NY))
            wait_recv(theirs, wx_r.at[d, e])

    slot = jnp.where(block_of_heads == mp, 0, 1)

    def part_copy(h, c):
        device = (t - core + c, block_of_heads)
        mine = (block_of_heads == mp) & (core == c)
        return mine, remote(part.at[h, c], arrived.at[h, slot], rs_s.at[h, c], rs_r.at[h, slot], device)

    def share(h):
        total = jnp.zeros((2 * TOK, HD), jnp.float32)
        for i in range(2):
            total = total + jnp.dot(
                gall[i].reshape(2 * TOK, K_DEV),
                wbuf[h, i * K_DEV : (i + 1) * K_DEV, :],
                preferred_element_type=jnp.float32,
            )
        part[h] = total.reshape(2, TOK, HD).astype(jnp.bfloat16)
        for c in range(2):
            mine, copy = part_copy(h, c)

            @pl.when(mine)
            def _():
                pltpu.make_async_copy(part.at[h, c], arrived.at[h, slot], rs_r.at[h, slot]).start()

            @pl.when(jnp.logical_not(mine))
            def _():
                copy.start()

    share(0)
    share(1)
    share(2)

    halo_columns(0)
    loads[4].wait()

    def softmax(h):
        wait_recv(win.at[h, :, 3], kvew_r.at[h, 0])
        wait_recv(win.at[h, :, 0], kvew_r.at[h, 1])
        keys = win[h, 0].reshape(KEYS, HD)
        for i in range(2):
            rows = slice(i * CHUNK, (i + 1) * CHUNK)
            scores = lax.dot_general(
                keys, q[rows, h * HD : (h + 1) * HD], LAST, preferred_element_type=jnp.float32
            )
            scores = scores * (SCALE * LOG2E) + bias[...]
            unnormed = jnp.exp2(scores - jnp.max(scores, axis=0, keepdims=True))
            prob[h, i] = unnormed * (1.0 / jnp.sum(unnormed, axis=0, keepdims=True))

    def spread_columns(h):
        send(ew_out.at[h, 0], ew_in.at[h, 0], dew_s.at[h, 0], dew_r.at[h, 0], west)
        send(ew_out.at[h, 1], ew_in.at[h, 1], dew_s.at[h, 1], dew_r.at[h, 1], east)

    def spread_rows(h):
        wait_recv(ew_in.at[h, 0], dew_r.at[h, 0])
        wait_recv(ew_in.at[h, 1], dew_r.at[h, 1])
        for kv in range(2):
            dwin[h, kv, 2] = dwin[h, kv, 2] + ew_in[h, 0, kv].astype(jnp.float32)
            dwin[h, kv, 1] = dwin[h, kv, 1] + ew_in[h, 1, kv].astype(jnp.float32)
            for i in range(2):
                ns_out[h, 0, kv, i] = dwin[h, kv, 1 + i, 0:STRIP].astype(jnp.bfloat16)
                ns_out[h, 1, kv, i] = dwin[h, kv, 1 + i, 3 * STRIP : 4 * STRIP].astype(jnp.bfloat16)
        send(ns_out.at[h, 0], ns_in.at[h, 0], dns_s.at[h, 0], dns_r.at[h, 0], north)
        send(ns_out.at[h, 1], ns_in.at[h, 1], dns_s.at[h, 1], dns_r.at[h, 1], south)

    def backward(h):
        lanes = slice(h * HD, (h + 1) * HD)
        total = jnp.zeros((TOK, HD), jnp.float32)
        for s in range(2):
            wait_recv(arrived.at[h, s], rs_r.at[h, s])
            total = total + arrived[h, s].astype(jnp.float32)
        cotangent = total.astype(jnp.bfloat16)
        keys = win[h, 0].reshape(KEYS, HD)
        values = win[h, 1].reshape(KEYS, HD)
        for i in range(2):
            rows = slice(i * CHUNK, (i + 1) * CHUNK)
            attention = prob[h, i]
            grad_attention = lax.dot_general(
                values, cotangent[rows], LAST, preferred_element_type=jnp.float32
            )
            row_total = jnp.sum(attention * grad_attention, axis=0, keepdims=True)
            grad_s[:, rows] = (attention * (grad_attention - row_total) * SCALE).astype(jnp.bfloat16)
            prob_low[:, rows] = attention.astype(jnp.bfloat16)
        dwin[h, 0] = jnp.dot(
            grad_s[...], q[:, lanes], preferred_element_type=jnp.float32
        ).reshape(4, 256, HD)
        dwin[h, 1] = jnp.dot(
            prob_low[...], cotangent, preferred_element_type=jnp.float32
        ).reshape(4, 256, HD)
        for kv in range(2):
            ew_out[h, 0, kv] = dwin[h, kv, 0].astype(jnp.bfloat16)
            ew_out[h, 1, kv] = dwin[h, kv, 3].astype(jnp.bfloat16)
        spread_columns(h)
        dq_ref[:, lanes] = lax.dot_general(
            grad_s[...], keys, FIRST, preferred_element_type=jnp.float32
        ).astype(jnp.bfloat16)

    def finish(h):
        wait_recv(ns_in.at[h, 0], dns_r.at[h, 0])
        wait_recv(ns_in.at[h, 1], dns_r.at[h, 1])
        for kv, ref in enumerate((dk_ref, dv_ref)):
            halves = []
            for i in range(2):
                upper = dwin[h, kv, 1 + i, STRIP : 2 * STRIP] + ns_in[h, 1, kv, i].astype(jnp.float32)
                lower = dwin[h, kv, 1 + i, 2 * STRIP : 3 * STRIP] + ns_in[h, 0, kv, i].astype(jnp.float32)
                halves.append(jnp.concatenate([upper, lower], axis=0).reshape(16, 8, HD))
            ref[:, h * HD : (h + 1) * HD] = jnp.stack(halves, axis=1).reshape(TOK, HD).astype(jnp.bfloat16)

    softmax(0)
    halo_columns(1)
    backward(0)
    softmax(1)
    halo_columns(2)
    spread_rows(0)
    backward(1)
    softmax(2)
    spread_rows(1)
    backward(2)
    spread_rows(2)
    for h in range(HEADS_DEV - 1):
        finish(h)

    for copy in sent[:-2]:
        copy.wait_send()
    for hi in range(2):
        device = scatter_to[hi]
        mine = (device[0] == t) & (device[1] == mp)

        @pl.when(jnp.logical_not(mine))
        def _():
            remote(wpad, stage.at[core], wsc_s.at[hi], wsc_r.at[core], device).wait_send()

    for h in range(HEADS_DEV):
        for c in range(2):
            mine, copy = part_copy(h, c)

            @pl.when(jnp.logical_not(mine))
            def _():
                copy.wait_send()

    finish(HEADS_DEV - 1)
    for copy in sent[-2:]:
        copy.wait_send()


def hand_over(a, b, c, a_out, b_out, c_out, sem):
    copies = [
        pltpu.make_async_copy(src, dst, sem.at[i])
        for i, (src, dst) in enumerate(((a, a_out), (b, b_out), (c, c_out)))
    ]
    for copy in copies:
        copy.start()
    for copy in copies:
        copy.wait()


def shards(query, key, value, grad_y, w_out):
    bf16, f32 = jnp.bfloat16, jnp.float32
    dma = pltpu.SemaphoreType.DMA
    out = jax.ShapeDtypeStruct(query.shape, bf16)
    held = pltpu.VMEM(query.shape, bf16)
    vmem = pl.BlockSpec(memory_space=pltpu.VMEM)
    hbm = pl.BlockSpec(memory_space=pltpu.HBM)
    grads = pl.pallas_call(
        kernel,
        name="tiled_attention_backward",
        out_shape=(held, held, held),
        in_specs=[hbm] * 5,
        out_specs=(vmem,) * 3,
        scratch_shapes=[
            pltpu.VMEM((HEADS_DEV, 2, 4, 256, HD), bf16),
            pltpu.VMEM((32, HEADS_DEV * HD), bf16),
            pltpu.VMEM((2, 32, HEADS_DEV * HD), bf16),
            pltpu.VMEM((HEADS_DEV, K_PAIR, HD), bf16),
            pltpu.VMEM((2, 2, TOK, K_DEV), bf16),
            pltpu.VMEM((HEADS_DEV, 2, TOK, HD), bf16),
            pltpu.VMEM((HEADS_DEV, 2, TOK, HD), bf16),
            pltpu.VMEM((KEYS, CHUNK), f32),
            pltpu.VMEM((HEADS_DEV, 2, KEYS, CHUNK), f32),
            pltpu.VMEM((KEYS, TOK), bf16),
            pltpu.VMEM((KEYS, TOK), bf16),
            pltpu.VMEM((HEADS_DEV, 2, 4, 256, HD), f32),
            pltpu.VMEM((HEADS_DEV, 2, 2, 256, HD), bf16),
            pltpu.VMEM((HEADS_DEV, 2, 2, 256, HD), bf16),
            pltpu.VMEM((HEADS_DEV, 2, 2, 2, STRIP, HD), bf16),
            pltpu.VMEM((HEADS_DEV, 2, 2, 2, STRIP, HD), bf16),
            pltpu.VMEM(query.shape, bf16),
            pltpu.VMEM(key.shape, bf16),
            pltpu.VMEM(value.shape, bf16),
            dma((HEADS_DEV, 2)), dma((HEADS_DEV, 2)),
            dma((HEADS_DEV, 2)), dma((HEADS_DEV, 2)),
            dma((2,)), dma((2,)),
            dma((3,)), dma((3,)),
            dma((NY,)), dma((NY,)),
            dma((NY, NX)), dma((NY, NX)),
            dma((HEADS_DEV, 2)), dma((HEADS_DEV, 2)),
            dma((HEADS_DEV, 2)), dma((HEADS_DEV, 2)),
            dma((HEADS_DEV, 2)), dma((HEADS_DEV, 2)),
            dma((5,)),
        ],
        compiler_params=pltpu.CompilerParams(
            collective_id=0, has_side_effects=True, vmem_limit_bytes=60 * 1024 * 1024
        ),
    )(query, key, value, grad_y, jnp.pad(w_out, ((0, 8), (0, 0))))
    return pl.pallas_call(
        hand_over,
        name="hand_over",
        out_shape=(out, out, out),
        in_specs=[vmem] * 3,
        out_specs=(hbm,) * 3,
        scratch_shapes=[dma((3,))],
    )(*(pltpu.with_memory_space_constraint(g, pltpu.VMEM) for g in grads))


def solution(mesh):
    spec = P("tile", "mp")
    return jax.shard_map(
        shards, mesh=mesh, in_specs=(spec,) * 5, out_specs=(spec,) * 3, check_vma=False
    )
```

```python
import jax
import jax.numpy as jnp
from jax import lax
from jax.experimental import pallas as pl
from jax.experimental.pallas import tpu as pltpu
from jax.sharding import PartitionSpec as P

HD = 128
HEADS_DEV = 3
COLUMNS = 8
ROWS = 16
NY = 8
NX = 4
TOK = 256
STRIP = 64
KEYS = 1024
CHUNK = 128
K_DEV = 768
K_PAIR = 1536
LOG2E = 1.4426950408889634
SCALE = HD ** (-0.5)
MESH = pl.DeviceIdType.MESH
LAST = (((1,), (1,)), ((), ()))
FIRST = (((0,), (0,)), ((), ()))


def tile_of(x, y, z_hi, core):
    return ((y * 2 + z_hi) * NX + x) * 2 + core


def held_block(y, mp):
    p = lax.rem(y - 4 * (mp // 2) + NY, NY)
    return jnp.where(p < 4, p, 7 - p), jnp.where(p < 4, 0, 1)


def to_halves(tokens):
    wide = tokens.astype(jnp.float32).reshape(16, 2, 8, HD)
    return [wide[:, i].reshape(128, HD).astype(jnp.bfloat16) for i in range(2)]


def kernel(
    q_hbm, k_hbm, v_hbm, g_hbm, w_ref, dq_ref, dk_ref, dv_ref,
    win, wpad, stage, wbuf, gall, part, arrived, bias, prob, grad_s, prob_low, dwin,
    ew_out, ew_in, ns_out, ns_in, q, k, v,
    kvns_s, kvns_r, kvew_s, kvew_r, wsc_s, wsc_r, g_s, g_r, wy_s, wy_r, wx_s, wx_r,
    rs_s, rs_r, dew_s, dew_r, dns_s, dns_r, load,
):
    t = lax.axis_index("tile")
    mp = lax.axis_index("mp")
    core = lax.rem(t, 2)
    x = lax.rem(t // 2, NX)
    z_hi = lax.rem(t // COLUMNS, 2)
    y = t // (2 * COLUMNS)
    row = t // COLUMNS
    col = lax.rem(t, COLUMNS)
    north = (lax.rem(t + 128 - COLUMNS, 128), mp)
    south = (lax.rem(t + COLUMNS, 128), mp)
    east = (row * COLUMNS + lax.rem(col + 1, COLUMNS), mp)
    west = (row * COLUMNS + lax.rem(col + 7, COLUMNS), mp)
    other = (t + 1 - 2 * core, mp)

    half, within = y // 4, lax.rem(y, 4)
    y_to = jnp.where(z_hi == 0, y, lax.rem(4 * half + 7 - within, NY))
    scatter_to = [(tile_of(x, y_to, hi, mp // 2), 2 * half + lax.rem(mp, 2)) for hi in range(2)]
    b_in, b_hi = held_block(y, mp)
    scatter_from = [
        (tile_of(x, 4 * (mp // 2) + b_in, b_hi, c), lax.rem(mp, 2) + 2 * core) for c in range(2)
    ]
    side = lax.rem(mp, 2)
    pair = mp + 1 - 2 * side
    far = lax.rem(mp + 2, 4)
    block_of_heads = side + 2 * core

    def y_peer(d):
        return (tile_of(x, lax.rem(y + d, NY), z_hi, core), mp)

    def x_peer(e):
        return (tile_of(lax.rem(x + e, NX), y, z_hi, core), mp)

    greeted = [north, south, east, west] + scatter_to + scatter_from
    greeted += [y_peer(d) for d in range(1, NY)] + [x_peer(e) for e in range(1, NX)]
    greeted += [(t, pair), (t, far), (other[0], far)]
    barrier = pltpu.get_barrier_semaphore()
    for device in greeted:
        pl.semaphore_signal(barrier, inc=1, device_id=device, device_id_type=MESH)

    loads = []
    for i, (src, dst) in enumerate(
        ((k_hbm, k), (v_hbm, v), (g_hbm, gall.at[side, core]), (q_hbm, q))
    ):
        loads.append(pltpu.make_async_copy(src, dst, load.at[i]))
        loads[-1].start()

    wpad[0:24, :] = w_ref[...]
    wpad[24:32, :] = jnp.zeros((8, HEADS_DEV * HD), jnp.bfloat16)
    loads[0].wait()
    loads[1].wait()
    for h in range(HEADS_DEV):
        lanes = slice(h * HD, (h + 1) * HD)
        for kv, ref in enumerate((k, v)):
            halves = to_halves(ref[:, lanes])
            for i in range(2):
                win[h, kv, 1 + i, STRIP : STRIP + 128, :] = halves[i]
    loads[2].wait()
    pl.semaphore_wait(barrier, len(greeted))

    def remote(src, dst, send, recv, device):
        return pltpu.make_async_remote_copy(src, dst, send, recv, device_id=device, device_id_type=MESH)

    sent = []

    def send(src, dst, send_sem, recv_sem, device):
        copy = remote(src, dst, send_sem, recv_sem, device)
        copy.start()
        sent.append(copy)

    def wait_recv(dst, recv_sem):
        remote(dst, dst, recv_sem, recv_sem, other).wait_recv()

    for hi in range(2):
        device = scatter_to[hi]
        mine = (device[0] == t) & (device[1] == mp)

        @pl.when(mine)
        def _():
            pltpu.make_async_copy(wpad, stage.at[core], wsc_r.at[core]).start()

        @pl.when(jnp.logical_not(mine))
        def _():
            remote(wpad, stage.at[core], wsc_s.at[hi], wsc_r.at[core], device).start()

    def top(h):
        return win.at[h, :, 1:3, STRIP : 2 * STRIP]

    def bottom(h):
        return win.at[h, :, 1:3, 2 * STRIP : 3 * STRIP]

    def halo_n(h):
        return win.at[h, :, 1:3, 0:STRIP]

    def halo_s(h):
        return win.at[h, :, 1:3, 3 * STRIP : 4 * STRIP]

    mine_g = gall.at[side, core]
    near_g = gall.at[1 - side, core]
    send(mine_g, mine_g, g_s.at[0], g_r.at[0], (t, pair))
    send(mine_g, mine_g, g_s.at[1], g_r.at[1], other)

    def halo_rows(h):
        send(top(h), halo_s(h), kvns_s.at[h, 0], kvns_r.at[h, 0], north)
        send(bottom(h), halo_n(h), kvns_s.at[h, 1], kvns_r.at[h, 1], south)

    def halo_columns(h):
        wait_recv(halo_s(h), kvns_r.at[h, 0])
        wait_recv(halo_n(h), kvns_r.at[h, 1])
        send(win.at[h, :, 1], win.at[h, :, 3], kvew_s.at[h, 0], kvew_r.at[h, 0], west)
        send(win.at[h, :, 2], win.at[h, :, 0], kvew_s.at[h, 1], kvew_r.at[h, 1], east)

    halo_rows(0)
    halo_rows(1)

    key_at = lax.broadcasted_iota(jnp.int32, (KEYS, CHUNK), 0)
    group = key_at // 256
    key_row = lax.rem(key_at, 256) // 8
    valid = (
        ((group > 0) | (col > 0))
        & ((group < 3) | (col < COLUMNS - 1))
        & ((key_row >= 8) | (row > 0))
        & ((key_row < 24) | (row < ROWS - 1))
    )
    bias[...] = jnp.where(valid, 0.0, -1e30)

    for c in range(2):
        wait_recv(stage.at[c], wsc_r.at[c])

    def block_at(x_at, y_at):
        inside, hi = held_block(y_at, mp)
        begin = pl.multiple_of(48 * ((inside * 2 + hi) * NX + x_at), 16)
        return wbuf.at[:, pl.ds(begin, 48), :]

    block = stage[:, 0:24, :].astype(jnp.float32).reshape(48, HEADS_DEV * HD).astype(jnp.bfloat16)
    begin = pl.multiple_of(48 * ((b_in * 2 + b_hi) * NX + x), 16)
    for h in range(HEADS_DEV):
        wbuf[h, pl.ds(begin, 48), :] = block[:, h * HD : (h + 1) * HD]
    my_block = block_at(x, y)
    y_order = (1, 7, 2, 6, 3, 5, 4)
    x_order = (1, 3, 2)
    for d in y_order:
        send(my_block, my_block, wy_s.at[d], wy_r.at[d], y_peer(d))
    for e in x_order:
        send(my_block, my_block, wx_s.at[0, e], wx_r.at[0, e], x_peer(e))
    for d in y_order:
        theirs = block_at(x, lax.rem(y + NY - d, NY))
        wait_recv(theirs, wy_r.at[d])
        for e in x_order:
            send(theirs, theirs, wx_s.at[d, e], wx_r.at[d, e], x_peer(e))
    halo_rows(2)

    wait_recv(near_g, g_r.at[0])
    send(near_g, near_g, g_s.at[2], g_r.at[2], other)
    wait_recv(gall.at[side, 1 - core], g_r.at[1])
    wait_recv(gall.at[1 - side, 1 - core], g_r.at[2])

    for d in (0,) + y_order:
        for e in x_order:
            theirs = block_at(lax.rem(x + NX - e, NX), lax.rem(y + NY - d, NY))
            wait_recv(theirs, wx_r.at[d, e])

    slot = jnp.where(block_of_heads == mp, 0, 1)

    def part_copy(h, c):
        device = (t - core + c, block_of_heads)
        mine = (block_of_heads == mp) & (core == c)
        return mine, remote(part.at[h, c], arrived.at[h, slot], rs_s.at[h, c], rs_r.at[h, slot], device)

    def share(h):
        total = jnp.zeros((2 * TOK, HD), jnp.float32)
        for i in range(2):
            total = total + jnp.dot(
                gall[i].reshape(2 * TOK, K_DEV),
                wbuf[h, i * K_DEV : (i + 1) * K_DEV, :],
                preferred_element_type=jnp.float32,
            )
        part[h] = total.reshape(2, TOK, HD).astype(jnp.bfloat16)
        for c in range(2):
            mine, copy = part_copy(h, c)

            @pl.when(mine)
            def _():
                pltpu.make_async_copy(part.at[h, c], arrived.at[h, slot], rs_r.at[h, slot]).start()

            @pl.when(jnp.logical_not(mine))
            def _():
                copy.start()

    share(0)
    share(1)
    share(2)

    halo_columns(0)
    loads[3].wait()

    def softmax(h):
        wait_recv(win.at[h, :, 3], kvew_r.at[h, 0])
        wait_recv(win.at[h, :, 0], kvew_r.at[h, 1])
        keys = win[h, 0].reshape(KEYS, HD)
        for i in range(2):
            rows = slice(i * CHUNK, (i + 1) * CHUNK)
            scores = lax.dot_general(
                keys, q[rows, h * HD : (h + 1) * HD], LAST, preferred_element_type=jnp.float32
            )
            scores = scores * (SCALE * LOG2E) + bias[...]
            unnormed = jnp.exp2(scores - jnp.max(scores, axis=0, keepdims=True))
            prob[h, i] = unnormed * (1.0 / jnp.sum(unnormed, axis=0, keepdims=True))

    def spread_columns(h):
        send(ew_out.at[h, 0], ew_in.at[h, 0], dew_s.at[h, 0], dew_r.at[h, 0], west)
        send(ew_out.at[h, 1], ew_in.at[h, 1], dew_s.at[h, 1], dew_r.at[h, 1], east)

    def spread_rows(h):
        wait_recv(ew_in.at[h, 0], dew_r.at[h, 0])
        wait_recv(ew_in.at[h, 1], dew_r.at[h, 1])
        for kv in range(2):
            dwin[h, kv, 2] = dwin[h, kv, 2] + ew_in[h, 0, kv].astype(jnp.float32)
            dwin[h, kv, 1] = dwin[h, kv, 1] + ew_in[h, 1, kv].astype(jnp.float32)
            for i in range(2):
                ns_out[h, 0, kv, i] = dwin[h, kv, 1 + i, 0:STRIP].astype(jnp.bfloat16)
                ns_out[h, 1, kv, i] = dwin[h, kv, 1 + i, 3 * STRIP : 4 * STRIP].astype(jnp.bfloat16)
        send(ns_out.at[h, 0], ns_in.at[h, 0], dns_s.at[h, 0], dns_r.at[h, 0], north)
        send(ns_out.at[h, 1], ns_in.at[h, 1], dns_s.at[h, 1], dns_r.at[h, 1], south)

    def backward(h):
        lanes = slice(h * HD, (h + 1) * HD)
        total = jnp.zeros((TOK, HD), jnp.float32)
        for s in range(2):
            wait_recv(arrived.at[h, s], rs_r.at[h, s])
            total = total + arrived[h, s].astype(jnp.float32)
        cotangent = total.astype(jnp.bfloat16)
        keys = win[h, 0].reshape(KEYS, HD)
        values = win[h, 1].reshape(KEYS, HD)
        for i in range(2):
            rows = slice(i * CHUNK, (i + 1) * CHUNK)
            attention = prob[h, i]
            grad_attention = lax.dot_general(
                values, cotangent[rows], LAST, preferred_element_type=jnp.float32
            )
            row_total = jnp.sum(attention * grad_attention, axis=0, keepdims=True)
            grad_s[:, rows] = (attention * (grad_attention - row_total) * SCALE).astype(jnp.bfloat16)
            prob_low[:, rows] = attention.astype(jnp.bfloat16)
        dwin[h, 0] = jnp.dot(
            grad_s[...], q[:, lanes], preferred_element_type=jnp.float32
        ).reshape(4, 256, HD)
        dwin[h, 1] = jnp.dot(
            prob_low[...], cotangent, preferred_element_type=jnp.float32
        ).reshape(4, 256, HD)
        for kv in range(2):
            ew_out[h, 0, kv] = dwin[h, kv, 0].astype(jnp.bfloat16)
            ew_out[h, 1, kv] = dwin[h, kv, 3].astype(jnp.bfloat16)
        spread_columns(h)
        dq_ref[:, lanes] = lax.dot_general(
            grad_s[...], keys, FIRST, preferred_element_type=jnp.float32
        ).astype(jnp.bfloat16)

    def finish(h):
        wait_recv(ns_in.at[h, 0], dns_r.at[h, 0])
        wait_recv(ns_in.at[h, 1], dns_r.at[h, 1])
        for kv, ref in enumerate((dk_ref, dv_ref)):
            halves = []
            for i in range(2):
                upper = dwin[h, kv, 1 + i, STRIP : 2 * STRIP] + ns_in[h, 1, kv, i].astype(jnp.float32)
                lower = dwin[h, kv, 1 + i, 2 * STRIP : 3 * STRIP] + ns_in[h, 0, kv, i].astype(jnp.float32)
                halves.append(jnp.concatenate([upper, lower], axis=0).reshape(16, 8, HD))
            ref[:, h * HD : (h + 1) * HD] = jnp.stack(halves, axis=1).reshape(TOK, HD).astype(jnp.bfloat16)

    softmax(0)
    halo_columns(1)
    backward(0)
    softmax(1)
    halo_columns(2)
    spread_rows(0)
    backward(1)
    softmax(2)
    spread_rows(1)
    backward(2)
    spread_rows(2)
    for h in range(HEADS_DEV - 1):
        finish(h)

    for copy in sent[:-2]:
        copy.wait_send()
    for hi in range(2):
        device = scatter_to[hi]
        mine = (device[0] == t) & (device[1] == mp)

        @pl.when(jnp.logical_not(mine))
        def _():
            remote(wpad, stage.at[core], wsc_s.at[hi], wsc_r.at[core], device).wait_send()

    for h in range(HEADS_DEV):
        for c in range(2):
            mine, copy = part_copy(h, c)

            @pl.when(jnp.logical_not(mine))
            def _():
                copy.wait_send()

    finish(HEADS_DEV - 1)
    for copy in sent[-2:]:
        copy.wait_send()


def hand_over(a, b, c, a_out, b_out, c_out, sem):
    copies = [
        pltpu.make_async_copy(src, dst, sem.at[i])
        for i, (src, dst) in enumerate(((a, a_out), (b, b_out), (c, c_out)))
    ]
    for copy in copies:
        copy.start()
    for copy in copies:
        copy.wait()


def shards(query, key, value, grad_y, w_out):
    bf16, f32 = jnp.bfloat16, jnp.float32
    dma = pltpu.SemaphoreType.DMA
    out = jax.ShapeDtypeStruct(query.shape, bf16)
    held = pltpu.VMEM(query.shape, bf16)
    vmem = pl.BlockSpec(memory_space=pltpu.VMEM)
    hbm = pl.BlockSpec(memory_space=pltpu.HBM)
    grads = pl.pallas_call(
        kernel,
        name="tiled_attention_backward",
        out_shape=(held, held, held),
        in_specs=[hbm] * 4 + [vmem],
        out_specs=(vmem,) * 3,
        scratch_shapes=[
            pltpu.VMEM((HEADS_DEV, 2, 4, 256, HD), bf16),
            pltpu.VMEM((32, HEADS_DEV * HD), bf16),
            pltpu.VMEM((2, 32, HEADS_DEV * HD), bf16),
            pltpu.VMEM((HEADS_DEV, K_PAIR, HD), bf16),
            pltpu.VMEM((2, 2, TOK, K_DEV), bf16),
            pltpu.VMEM((HEADS_DEV, 2, TOK, HD), bf16),
            pltpu.VMEM((HEADS_DEV, 2, TOK, HD), bf16),
            pltpu.VMEM((KEYS, CHUNK), f32),
            pltpu.VMEM((HEADS_DEV, 2, KEYS, CHUNK), f32),
            pltpu.VMEM((KEYS, TOK), bf16),
            pltpu.VMEM((KEYS, TOK), bf16),
            pltpu.VMEM((HEADS_DEV, 2, 4, 256, HD), f32),
            pltpu.VMEM((HEADS_DEV, 2, 2, 256, HD), bf16),
            pltpu.VMEM((HEADS_DEV, 2, 2, 256, HD), bf16),
            pltpu.VMEM((HEADS_DEV, 2, 2, 2, STRIP, HD), bf16),
            pltpu.VMEM((HEADS_DEV, 2, 2, 2, STRIP, HD), bf16),
            pltpu.VMEM(query.shape, bf16),
            pltpu.VMEM(key.shape, bf16),
            pltpu.VMEM(value.shape, bf16),
            dma((HEADS_DEV, 2)), dma((HEADS_DEV, 2)),
            dma((HEADS_DEV, 2)), dma((HEADS_DEV, 2)),
            dma((2,)), dma((2,)),
            dma((3,)), dma((3,)),
            dma((NY,)), dma((NY,)),
            dma((NY, NX)), dma((NY, NX)),
            dma((HEADS_DEV, 2)), dma((HEADS_DEV, 2)),
            dma((HEADS_DEV, 2)), dma((HEADS_DEV, 2)),
            dma((HEADS_DEV, 2)), dma((HEADS_DEV, 2)),
            dma((4,)),
        ],
        compiler_params=pltpu.CompilerParams(
            collective_id=0, has_side_effects=True, vmem_limit_bytes=60 * 1024 * 1024
        ),
    )(query, key, value, grad_y, pltpu.with_memory_space_constraint(w_out, pltpu.VMEM))
    return pl.pallas_call(
        hand_over,
        name="hand_over",
        out_shape=(out, out, out),
        in_specs=[vmem] * 3,
        out_specs=(hbm,) * 3,
        scratch_shapes=[dma((3,))],
    )(*(pltpu.with_memory_space_constraint(g, pltpu.VMEM) for g in grads))


def solution(mesh):
    spec = P("tile", "mp")
    return jax.shard_map(
        shards, mesh=mesh, in_specs=(spec,) * 5, out_specs=(spec,) * 3, check_vma=False
    )
```
